32 devices in a mesh: dp: 8 (over z, y), ctx: 4 (over x, core).
Axes of the slice: x: 2, y: 2, z: 4, core: 2. Of those that a mesh axis runs over, the one named last changes fastest.
Arguments:
- tokens: bfloat16 [16, 2048, 960], P('dp', 'ctx'), may hold values from -6 to 6
- segments: int32 [16, 2048], P('dp', 'ctx'), may hold values from 0 to 34, as said below
- cotangent: float32 [16, 2048, 960], P('dp', 'ctx'), may hold values from -6 to 6
- attn_gain: bfloat16 [960], P('ctx'), may hold values from 0.5 to 1.5
- query_weight: bfloat16 [960, 960], P('dp', 'ctx'), may hold values from -0.1875 to 0.1875
- key_matrix: bfloat16 [960, 320], P('dp', 'ctx'), may hold values from -0.1875 to 0.1875
- value_matrix: bfloat16 [960, 320], P('dp', 'ctx'), may hold values from -0.1875 to 0.1875
- output_weight: bfloat16 [960, 960], P('dp', 'ctx'), may hold values from -1.25 to 1.25
- second_gain: bfloat16 [960], P('ctx'), may hold values from 0.5 to 1.5
- gate_weight: bfloat16 [960, 2560], P('dp', 'ctx'), may hold values from -0.1875 to 0.1875
- up_weight: bfloat16 [960, 2560], P('dp', 'ctx'), may hold values from -0.1875 to 0.1875
- down_weight: bfloat16 [2560, 960], P('dp', 'ctx'), may hold values from -0.125 to 0.125
Outputs:
- block_output: bfloat16 [16, 2048, 960], P('dp', 'ctx')
- input_grad: float32 [16, 2048, 960], P('dp', 'ctx')
- attn_gain_grad: float32 [960], P('ctx')
- query_grad: float32 [960, 960], P('dp', 'ctx')
- key_grad: float32 [960, 320], P('dp', 'ctx')
- value_grad: float32 [960, 320], P('dp', 'ctx')
- output_grad: float32 [960, 960], P('dp', 'ctx')
- second_gain_grad: float32 [960], P('ctx')
- gate_grad: float32 [960, 2560], P('dp', 'ctx')
- up_grad: float32 [960, 2560], P('dp', 'ctx')
- down_grad: float32 [2560, 960], P('dp', 'ctx')
The draws below stay inside these ranges and needn't reach their ends.
Inputs may be any that keep to these rules, and one draw needn't show every extreme that they name: `segments`: in each sequence the numbers start at 0 and rise by one at each document boundary; every document holds 60 to 800 tokens except that the last one of a sequence may be cut shorter; one sequence of the whole batch is cut into documents of exactly 60 tokens; every data index holds one other sequence that is a single document, except the data index of that cut sequence where 2 is 1.
All inputs are finite; a program needn't handle non-finite values.
Results may differ from the reference program's by a relative error of at most 0.022.
Values may be sent and summed in bfloat16 or wider, within the bound.
No kernel may reach another device: no remote copies, remote signals or barrier semaphores. Data moves between devices by JAX's collectives and lax.ppermute only.
A program may use at most 256 MiB of HBM per device.

```python
import math
import jax
import jax.numpy as jnp
from jax import lax

D = 960
QUERY_HEADS = 15
KEY_VALUE_HEADS = 5
HEAD_SIZE = 64
FF = 2560
SEQ_LEN = 2048
DOC_MIN = 60
DOC_MAX = 800
QD = 960
KVD = 320
SEQS = 2
NSEQ = 16


def draw_segments(key, part):
    key = jax.random.fold_in(key, 11)
    first_key, second_key, third_key = jax.random.split(key, 3)
    count_items = SEQ_LEN // DOC_MIN + 1
    lengths = jax.random.randint(first_key, (NSEQ, count_items), DOC_MIN, DOC_MAX + 1, dtype=jnp.int32)
    ends = jnp.cumsum(lengths, axis=1)
    places = jnp.arange(SEQ_LEN, dtype=jnp.int32)
    numbers = jnp.sum((ends[:, None, :] <= places[None, :, None]).astype(jnp.int32), axis=2)
    chosen = jax.random.randint(second_key, (NSEQ // SEQS,), 0, SEQS, dtype=jnp.int32)
    rows = jnp.arange(NSEQ, dtype=jnp.int32)
    single = chosen[rows // SEQS] == rows % SEQS
    group = jax.random.randint(third_key, (), 0, NSEQ // SEQS, dtype=jnp.int32)
    cut_row = group * SEQS + (chosen[group] + 1) % SEQS
    shortest = places // DOC_MIN
    result = jnp.where(single[:, None], 0, numbers)
    result = jnp.where((rows == cut_row)[:, None], shortest[None, :], result)
    return result.astype(jnp.int32)


def levels(stream_key, dims, cuts, low, top_value):
    factor_of = 1.0
    for axis_at, parts in cuts:
        heights = jax.random.uniform(jax.random.fold_in(jax.random.fold_in(stream_key, 6), axis_at), (parts,), jnp.float32, low / len(cuts), top_value / len(cuts))
        factor_of = factor_of * jnp.repeat(jnp.exp(heights), dims[axis_at] // parts).reshape((-1,) + (1,) * (len(dims) - 1 - axis_at))
    return factor_of


def gaussian(key, extent, scale, bound, cuts=(), held_as=jnp.bfloat16):
    values = jax.random.normal(key, extent, jnp.float32) * scale
    if len(cuts) > 0:
        values = levels(key, extent, cuts, -0.22, 0.18) * values
    return jnp.clip(values, min=-bound, max=bound).astype(held_as)


def setup_inputs(seed: int = 0) -> dict:
    seeds = jax.random.split(jax.random.key(seed), 13)
    tokens = gaussian(seeds[0], (NSEQ, SEQ_LEN, D), 1.0, 6.0, ((0, 8), (1, 4)))
    segments = draw_segments(jax.random.fold_in(seeds[12], 71), 0)
    cotangent = gaussian(seeds[2], (NSEQ, SEQ_LEN, D), 1.0, 6.0, ((0, 8), (1, 4)), jnp.float32)
    attn_gain = jnp.clip(1.0 + 0.1 * jax.random.normal(seeds[3], (D,), jnp.float32), 0.5, 1.5).astype(jnp.bfloat16)
    query_weight = gaussian(seeds[4], (D, QD), D ** -0.5, 0.1875, ((0, 8), (1, 4)))
    key_matrix = gaussian(seeds[5], (D, KVD), D ** -0.5, 0.1875, ((0, 8), (1, 4)))
    value_matrix = gaussian(seeds[6], (D, KVD), D ** -0.5, 0.1875, ((0, 8), (1, 4)))
    output_weight = gaussian(seeds[7], (QD, D), (max(QD // 48, 4)) ** -0.5, 1.25, ((0, 8), (1, 4)))
    second_gain = jnp.clip(1.0 + 0.1 * jax.random.normal(seeds[8], (D,), jnp.float32), 0.5, 1.5).astype(jnp.bfloat16)
    gate_weight = gaussian(seeds[9], (D, FF), D ** -0.5, 0.1875, ((0, 8), (1, 4)))
    up_weight = gaussian(seeds[10], (D, FF), D ** -0.5, 0.1875, ((0, 8), (1, 4)))
    down_weight = gaussian(seeds[11], (FF, D), FF ** -0.5, 0.125, ((0, 8), (1, 4)))
    return dict(tokens=tokens, segments=segments, cotangent=cotangent, attn_gain=attn_gain, query_weight=query_weight, key_matrix=key_matrix, value_matrix=value_matrix, output_weight=output_weight, second_gain=second_gain, gate_weight=gate_weight, up_weight=up_weight, down_weight=down_weight)


@jax.custom_vjp
def lower_precision(v):
    return lax.optimization_barrier(v.astype(jnp.bfloat16)).astype(jnp.float32)

@jax.custom_vjp
def lower_precision_backward(v):
    return v

def low_keep(v):
    return (lower_precision(v), None)

def low_pass(kept, grad):
    return (grad,)

def back_keep(v):
    return (v, None)

def back_low(kept, grad):
    return (lower_precision(grad),)
lower_precision.defvjp(low_keep, low_pass)
lower_precision_backward.defvjp(back_keep, back_low)

def matrix_product(left, right):
    return jnp.einsum('gld,df->glf', left, right, precision=lax.Precision.HIGHEST)

def rope_tables(length_tokens):
    place = jnp.arange(length_tokens, dtype=jnp.int32).astype(jnp.float32)
    freq = jnp.exp(-math.log(10000.0) * jnp.arange(HEAD_SIZE // 2, dtype=jnp.int32).astype(jnp.float32) * 2.0 / HEAD_SIZE)
    angle = place[:, None] * freq[None, :]
    return (jnp.cos(angle), jnp.sin(angle))

def rotate_halves(field, cosine_table, sine_table):
    first = field[..., :HEAD_SIZE // 2]
    second = field[..., HEAD_SIZE // 2:]
    cosine_table = cosine_table[None, :, None, :]
    sine_table = sine_table[None, :, None, :]
    return jnp.concatenate([first * cosine_table - second * sine_table, second * cosine_table + first * sine_table], axis=-1)

def forward(xin, segs, weights):
    attn_gain, query_weight, key_matrix, value_matrix, output_weight, second_gain, gate_weight, up_weight, down_weight = weights
    group_count = xin.shape[0]
    length_tokens = xin.shape[1]
    head_ratio = QUERY_HEADS // KEY_VALUE_HEADS
    cosine_table, sine_table = rope_tables(length_tokens)
    first_norm = xin * lax.rsqrt(lax.optimization_barrier(jnp.mean(xin * xin, axis=-1, keepdims=True)) + 1e-05) * attn_gain
    first_hidden = lower_precision(first_norm)
    query_rows = lower_precision(rotate_halves(lower_precision_backward(matrix_product(first_hidden, query_weight)).reshape(group_count, length_tokens, QUERY_HEADS, HEAD_SIZE), cosine_table, sine_table))
    key_rows = lower_precision(rotate_halves(lower_precision_backward(matrix_product(first_hidden, key_matrix)).reshape(group_count, length_tokens, KEY_VALUE_HEADS, HEAD_SIZE), cosine_table, sine_table))
    value_rows = lower_precision(lower_precision_backward(matrix_product(first_hidden, value_matrix))).reshape(group_count, length_tokens, KEY_VALUE_HEADS, HEAD_SIZE)
    block_entry = math.gcd(length_tokens, 512)
    count_items = length_tokens // block_entry
    query_block_list = jnp.moveaxis(query_rows.reshape(group_count, count_items, block_entry, KEY_VALUE_HEADS, head_ratio, HEAD_SIZE), 1, 0)
    seg_blocks = jnp.moveaxis(segs.reshape(group_count, count_items, block_entry), 1, 0)
    starts = jnp.arange(count_items, dtype=jnp.int32) * block_entry
    key_place = jnp.arange(length_tokens, dtype=jnp.int32)

    def attend(item):
        qblk, sblk, start = item
        qplace = start + jnp.arange(block_entry, dtype=jnp.int32)
        raw = lower_precision_backward(jnp.einsum('gqhrd,gkhd->ghrqk', qblk, key_rows, precision=lax.Precision.HIGHEST))
        allowed = (key_place[None, None, :] <= qplace[None, :, None]) & (sblk[:, :, None] == segs[:, None, :])
        scores = jnp.where(allowed[:, None, None], raw * HEAD_SIZE ** (-0.5), -jnp.inf)
        top = lax.optimization_barrier(jnp.max(scores, axis=-1, keepdims=True))
        weight = jnp.exp(scores - top)
        prob = lower_precision(weight / lax.optimization_barrier(jnp.sum(weight, axis=-1, keepdims=True)))
        mixed = jnp.einsum('ghrqk,gkhd->gqhrd', prob, value_rows, precision=lax.Precision.HIGHEST)
        return lower_precision(lower_precision_backward(mixed.reshape(group_count, block_entry, QUERY_HEADS * HEAD_SIZE)))
    pieces = lax.map(jax.checkpoint(attend), (query_block_list, seg_blocks, starts))
    attended = jnp.moveaxis(pieces, 0, 1).reshape(group_count, length_tokens, QUERY_HEADS * HEAD_SIZE)
    after_attn = xin + lower_precision_backward(matrix_product(attended, output_weight))
    second_norm = after_attn * lax.rsqrt(lax.optimization_barrier(jnp.mean(after_attn * after_attn, axis=-1, keepdims=True)) + 1e-05) * second_gain
    hidden_two = lower_precision(second_norm)
    gate = lower_precision_backward(matrix_product(hidden_two, gate_weight))
    upward = lower_precision_backward(matrix_product(hidden_two, up_weight))
    inner = lower_precision(jax.nn.silu(gate) * upward)
    return after_attn + lower_precision_backward(matrix_product(inner, down_weight))

def reference(tokens, segments, cotangent, attn_gain, query_weight, key_matrix, value_matrix, output_weight, second_gain, gate_weight, up_weight, down_weight):
    weights = tuple((w.astype(jnp.float32) for w in (attn_gain, query_weight, key_matrix, value_matrix, output_weight, second_gain, gate_weight, up_weight, down_weight)))
    total = tokens.shape[0]
    per = math.gcd(total, max(1, 4096 // SEQ_LEN))
    rounds = total // per
    inputs = tokens.astype(jnp.float32).reshape(rounds, per, SEQ_LEN, D)
    seg_rows = segments.reshape(rounds, per, SEQ_LEN)
    grads_in = cotangent.reshape(rounds, per, SEQ_LEN, D)

    def step(sums, item):
        xblk, sblk, cblk = item

        def run(xvalue, *wvalues):
            return forward(xvalue, sblk, wvalues)
        yblk, pull = jax.vjp(run, xblk, *weights)
        grads = pull(cblk)
        sums = tuple((a + b for a, b in zip(sums, grads[1:])))
        return (sums, (yblk.astype(jnp.bfloat16), grads[0]))
    init = tuple((jnp.zeros_like(w) for w in weights))
    sums, (outputs, input_grads) = lax.scan(step, init, (inputs, seg_rows, grads_in))
    return (outputs.reshape(total, SEQ_LEN, D), input_grads.reshape(total, SEQ_LEN, D), sums[0], sums[1], sums[2], sums[3], sums[4], sums[5], sums[6], sums[7], sums[8])
```

```python
import functools
import math

import jax
import jax.numpy as jnp
from jax import lax
from jax.experimental import pallas as pl
from jax.experimental.pallas import tpu as pltpu
from jax.sharding import PartitionSpec as P

HEAD_SIZE = 64
HALF = HEAD_SIZE // 2
LOW = -1e30
F32 = jnp.float32
BF16 = jnp.bfloat16


def rope_tables(first, count_items):
    place = (first + jnp.arange(count_items, dtype=jnp.int32)).astype(F32)
    freq = jnp.exp(-math.log(10000.0) * jnp.arange(HALF, dtype=jnp.int32).astype(F32) * 2.0 / HEAD_SIZE)
    angle = freq[:, None] * place[None, :]
    return (jnp.cos(angle), jnp.sin(angle))


def rotate_rows(field, cosine, sine):
    seqs, features, span = field.shape
    parts = field.reshape(seqs, features // HEAD_SIZE, 2, HALF, span)
    a, b = parts[:, :, 0], parts[:, :, 1]
    return jnp.stack([a * cosine - b * sine, b * cosine + a * sine], axis=2).reshape(field.shape)


def contract(left, right, axes):
    return lax.dot_general(left, right, ((axes[:1], axes[1:]), ((), ())), preferred_element_type=F32)


def side_by_side(ref, heads, tile, size):
    cut = pl.ds(tile * size, size)
    return jnp.concatenate([ref[0, g * HEAD_SIZE : (g + 1) * HEAD_SIZE, cut] for g in range(heads)], axis=1)


def allowed_keys(j, size, start, place):
    key = j * size + lax.broadcasted_iota(jnp.int32, (size, start.shape[1]), 0)
    return (key >= start) & (key <= place)


def attend_kernel(heads, size, bounds, q_ref, kv_ref, rows_ref, o_ref, lse_ref):
    seq = pl.program_id(0)
    tiles = q_ref.shape[2] // size
    for t in range(tiles):
        q = side_by_side(q_ref, heads, t, size) * BF16(HEAD_SIZE**-0.5)
        cut = pl.ds(t * size, size)
        start = jnp.concatenate([rows_ref[0, 0:1, cut]] * heads, axis=1)
        place = jnp.concatenate([rows_ref[0, 1:2, cut]] * heads, axis=1)

        def one(j, state, masked):
            top, total, acc = state
            s = contract(kv_ref[j, 0, 0, 0], q, (0, 0))
            if masked:
                s = jnp.where(allowed_keys(j, size, start, place), s, LOW)
            new = jnp.maximum(top, jnp.max(s, axis=0, keepdims=True))
            shrink = jnp.exp(top - new)
            p = jnp.exp(s - new)
            total = total * shrink + jnp.sum(p, axis=0, keepdims=True)
            acc = acc * shrink + contract(kv_ref[j, 0, 1, 0], p.astype(BF16), (1, 0))
            return (new, total, acc)

        lanes = heads * size
        state = (jnp.full((1, lanes), LOW, F32), jnp.zeros((1, lanes), F32), jnp.zeros((HEAD_SIZE, lanes), F32))
        lo, mid, diag = (bounds[3 * (seq * tiles + t) + k] for k in range(3))
        state = lax.fori_loop(lo, mid, lambda j, c: one(j, c, True), state)
        state = lax.fori_loop(mid, diag, lambda j, c: one(j, c, False), state)
        top, total, acc = one(diag, state, True)
        out = (acc / total).astype(BF16)
        lse = top + jnp.log(total)
        for g in range(heads):
            o_ref[0, g * HEAD_SIZE : (g + 1) * HEAD_SIZE, cut] = out[:, g * size : (g + 1) * size]
            lse_ref[0, 0, g : g + 1, cut] = lse[:, g * size : (g + 1) * size]


def back_kernel(heads, size, bounds, q_ref, kv_ref, rows_ref, o_ref, do_ref, lse_ref, cos_ref, sin_ref, dq_ref, dkv_ref, sums):
    seq = pl.program_id(0)
    tiles = q_ref.shape[2] // size
    sums[...] = jnp.zeros_like(sums)
    for t in range(tiles):
        q = side_by_side(q_ref, heads, t, size) * BF16(HEAD_SIZE**-0.5)
        do = side_by_side(do_ref, heads, t, size)
        o = side_by_side(o_ref, heads, t, size)
        delta = jnp.sum(do.astype(F32) * o.astype(F32), axis=0, keepdims=True)
        cut = pl.ds(t * size, size)
        start = jnp.concatenate([rows_ref[0, 0:1, cut]] * heads, axis=1)
        place = jnp.concatenate([rows_ref[0, 1:2, cut]] * heads, axis=1)
        lse = jnp.concatenate([lse_ref[0, 0, g : g + 1, cut] for g in range(heads)], axis=1)

        def one(j, dq, masked):
            k, v = kv_ref[j, 0, 0, 0], kv_ref[j, 0, 1, 0]
            p = jnp.exp(contract(k, q, (0, 0)) - lse)
            if masked:
                p = jnp.where(allowed_keys(j, size, start, place), p, 0.0)
            dp = contract(v, do, (0, 0))
            ds = (p * (dp - delta)).astype(BF16)
            sums[j, 0] += contract(q, ds, (1, 1))
            sums[j, 1] += contract(do, p.astype(BF16), (1, 1))
            return dq + contract(k, ds, (1, 0))

        dq = jnp.zeros((HEAD_SIZE, heads * size), F32)
        lo, mid, diag = (bounds[3 * (seq * tiles + t) + k] for k in range(3))
        dq = lax.fori_loop(lo, mid, lambda j, c: one(j, c, True), dq)
        dq = lax.fori_loop(mid, diag, lambda j, c: one(j, c, False), dq)
        dq = one(diag, dq, True) * (HEAD_SIZE**-0.5)
        cosine, sine = cos_ref[:, cut], sin_ref[:, cut]
        for g in range(heads):
            a = dq[:HALF, g * size : (g + 1) * size]
            b = dq[HALF:, g * size : (g + 1) * size]
            dq_ref[0, g * HEAD_SIZE : g * HEAD_SIZE + HALF, cut] = (a * cosine + b * sine).astype(BF16)
            dq_ref[0, g * HEAD_SIZE + HALF : (g + 1) * HEAD_SIZE, cut] = (b * cosine - a * sine).astype(BF16)
    for j in range(sums.shape[0]):
        for k in range(2):
            dkv_ref[j, 0, k, 0] = sums[j, k].astype(BF16)


def attention_specs(seqs, span, all_tiles, heads_kv, heads, size):
    wide = pl.BlockSpec((1, heads * HEAD_SIZE, span), lambda s, h, b: (s, h, 0))
    kv = pl.BlockSpec((all_tiles, 1, 2, 1, HEAD_SIZE, size), lambda s, h, b: (0, s, 0, h, 0, 0))
    rows = pl.BlockSpec((1, 2, span), lambda s, h, b: (s, 0, 0))
    lse = pl.BlockSpec((1, 1, heads, span), lambda s, h, b: (s, h, 0, 0))
    table = pl.BlockSpec((HALF, span), lambda s, h, b: (0, 0))
    return wide, kv, rows, lse, table


def attend(q, kv, rows, bounds, heads):
    seqs, features, span = q.shape
    all_tiles, _, _, heads_kv, _, size = kv.shape
    wide, kvs, rs, lse, _ = attention_specs(seqs, span, all_tiles, heads_kv, heads, size)
    return pl.pallas_call(
        functools.partial(attend_kernel, heads, size),
        grid_spec=pltpu.PrefetchScalarGridSpec(
            num_scalar_prefetch=1, grid=(seqs, heads_kv), in_specs=[wide, kvs, rs], out_specs=[wide, lse]
        ),
        out_shape=[jax.ShapeDtypeStruct(q.shape, BF16), jax.ShapeDtypeStruct((seqs, heads_kv, heads, span), F32)],
        compiler_params=pltpu.CompilerParams(vmem_limit_bytes=40 << 20),
        cost_estimate=pl.CostEstimate(flops=4 * seqs * features * span * span * 3, bytes_accessed=8 << 20, transcendentals=0),
        name="attend",
    )(bounds, q, kv, rows)


def attend_back(q, kv, rows, bounds, o, do, lse, cosine, sine, heads):
    seqs, features, span = q.shape
    all_tiles, _, _, heads_kv, _, size = kv.shape
    wide, kvs, rs, ls, table = attention_specs(seqs, span, all_tiles, heads_kv, heads, size)
    return pl.pallas_call(
        functools.partial(back_kernel, heads, size),
        grid_spec=pltpu.PrefetchScalarGridSpec(
            num_scalar_prefetch=1,
            grid=(seqs, heads_kv),
            in_specs=[wide, kvs, rs, wide, wide, ls, table, table],
            out_specs=[wide, kvs],
            scratch_shapes=[pltpu.VMEM((all_tiles, 2, HEAD_SIZE, size), F32)],
        ),
        out_shape=[jax.ShapeDtypeStruct(q.shape, BF16), jax.ShapeDtypeStruct(kv.shape, BF16)],
        compiler_params=pltpu.CompilerParams(vmem_limit_bytes=40 << 20),
        cost_estimate=pl.CostEstimate(flops=10 * seqs * features * span * span * 3, bytes_accessed=16 << 20, transcendentals=0),
        name="attend_back",
    )(bounds, q, kv, rows, o, do, lse, cosine, sine)


def gather_all(shard):
    whole = lax.all_gather(shard, ("ctx", "dp"), axis=0, tiled=True)
    return whole.reshape(lax.axis_size("ctx"), -1, shard.shape[1])


def scatter_all(terms):
    flat = terms.reshape(-1, terms.shape[2])
    return lax.psum_scatter(flat, ("ctx", "dp"), scatter_dimension=0, tiled=True).astype(F32)


def norm_back(dnorm, value, scale, gain):
    dgain = jnp.sum(dnorm * value * scale, axis=(0, 1))
    scaled = dnorm * gain
    dvalue = scale * (scaled - value * scale * scale * jnp.mean(scaled * value, axis=-1, keepdims=True))
    return (dvalue, dgain)


def ein(form, left, right):
    return jnp.einsum(form, left, right, preferred_element_type=F32)


def columns_of(blocks):
    return blocks.transpose(1, 0, 2).reshape(blocks.shape[1], -1)


def body(
    tokens, segments, cotangent, attn_gain, query_weight, key_matrix, value_matrix, output_weight, second_gain,
    gate_weight, up_weight, down_weight,
):
    parts = lax.axis_size("ctx")
    seqs, span, width = tokens.shape
    nq, nk = query_weight.shape[1], key_matrix.shape[1]
    nf = gate_weight.shape[1]
    heads_kv = nk * parts // HEAD_SIZE
    heads_q = nq * parts // HEAD_SIZE
    heads = heads_q // heads_kv
    size = math.gcd(span, 256)
    tiles = span // size

    gains = lax.all_gather(jnp.stack([attn_gain, second_gain]), "ctx", axis=1, tiled=True).astype(F32)
    segs_all = lax.all_gather(segments, "ctx", axis=1, tiled=True)
    first_weights = gather_all(jnp.concatenate([query_weight, key_matrix, value_matrix, output_weight], axis=1))
    pair_shard, down_shard, first_weights = lax.optimization_barrier(
        (jnp.concatenate([gate_weight, up_weight], axis=1), down_weight, first_weights)
    )
    pair = gather_all(pair_shard)
    down = gather_all(down_shard)
    gain_one, gain_two = gains[0], gains[1]

    q_full = columns_of(first_weights[:, :, :nq])
    k_full = columns_of(first_weights[:, :, nq : nq + nk])
    v_full = columns_of(first_weights[:, :, nq + nk : nq + 2 * nk])
    o_full = columns_of(first_weights[:, :, nq + 2 * nk :])

    first = lax.axis_index("ctx") * span
    cosine, sine = rope_tables(first, span)
    place = first + jnp.arange(span, dtype=jnp.int32)
    start = jnp.sum((segs_all[:, None, :] < segments[:, :, None]).astype(jnp.int32), axis=2)
    rows = jnp.stack([start, jnp.broadcast_to(place[None], start.shape)], axis=1)
    diag = place[::size] // size
    lo = start[:, ::size] // size
    mid = jnp.minimum((start[:, size - 1 :: size] + size - 1) // size, diag[None])
    bounds = jnp.stack([lo, mid, jnp.broadcast_to(diag[None], lo.shape)], axis=2).reshape(-1)

    inputs = tokens.astype(F32)
    scale_one = lax.rsqrt(jnp.mean(inputs * inputs, axis=-1, keepdims=True) + 1e-05)
    hidden_one = (inputs * scale_one * gain_one).astype(BF16)
    key = rotate_rows(ein("df,scd->sfc", k_full, hidden_one), cosine, sine).astype(BF16)
    value = ein("df,scd->sfc", v_full, hidden_one).astype(BF16)
    kv_own = jnp.concatenate([key, value], axis=1).reshape(seqs, 2 * heads_kv * HEAD_SIZE, tiles, size)
    kv_own = kv_own.transpose(2, 0, 1, 3)
    kv = lax.all_gather(kv_own, "ctx", axis=0, tiled=True)
    kv = kv.reshape(parts * tiles, seqs, 2, heads_kv, HEAD_SIZE, size)
    query = rotate_rows(ein("df,scd->sfc", q_full, hidden_one), cosine, sine).astype(BF16)

    attended, lse = attend(query, kv, rows, bounds, heads)

    after = inputs + ein("sfc,fd->scd", attended, o_full)
    scale_two = lax.rsqrt(jnp.mean(after * after, axis=-1, keepdims=True) + 1e-05)
    hidden_two = (after * scale_two * gain_two).astype(BF16)
    g_full = columns_of(pair[:, :, :nf])
    u_full = columns_of(pair[:, :, nf:])
    d_full = columns_of(down)
    gate = ein("scd,df->scf", hidden_two, g_full)
    upward = ein("scd,df->scf", hidden_two, u_full)
    sigma = jax.nn.sigmoid(gate)
    active = gate * sigma
    inner = (active * upward).astype(BF16)
    block_output = (after + ein("scf,fd->scd", inner, d_full)).astype(BF16)

    grad_low = cotangent.astype(BF16)
    grad_parts = grad_low.reshape(seqs, span, parts, width // parts)
    down_grad = scatter_all(ein("scf,scod->ofd", inner, grad_parts).astype(BF16))
    dinner = ein("scd,fd->scf", grad_low, d_full)
    dgate = (dinner * upward * sigma * (1.0 + gate * (1.0 - sigma))).astype(BF16)
    dup = (dinner * active).astype(BF16)
    gate_term = ein("scd,scof->odf", hidden_two, dgate.reshape(seqs, span, parts, nf)).astype(BF16)
    up_term = ein("scd,scof->odf", hidden_two, dup.reshape(seqs, span, parts, nf)).astype(BF16)
    dhidden_two = ein("scf,df->scd", dgate, g_full) + ein("scf,df->scd", dup, u_full)
    dnorm_two, second_term = norm_back(dhidden_two, after, scale_two, gain_two)
    dafter = cotangent + dnorm_two
    dattn = dafter.astype(BF16)
    dattn_parts = dattn.reshape(seqs, span, parts, width // parts)
    output_term = ein("sfc,scod->ofd", attended, dattn_parts).astype(BF16)
    wide_grads = scatter_all(jnp.concatenate([gate_term, up_term, output_term], axis=2))
    gate_grad, up_grad, output_grad = wide_grads[:, :nf], wide_grads[:, nf : 2 * nf], wide_grads[:, 2 * nf :]

    dattended = ein("fd,scd->sfc", o_full, dattn).astype(BF16)
    dquery, dkv = attend_back(query, kv, rows, bounds, attended, dattended, lse, cosine, sine, heads)
    dkv = dkv.reshape(parts * tiles, seqs, 2 * heads_kv * HEAD_SIZE, size)
    dkv = lax.psum_scatter(dkv, "ctx", scatter_dimension=0, tiled=True).astype(F32)
    dkv = dkv.transpose(1, 2, 0, 3).reshape(seqs, 2 * heads_kv * HEAD_SIZE, span)
    dkey = rotate_rows(dkv[:, : heads_kv * HEAD_SIZE], cosine, -sine).astype(BF16)
    dvalue = dkv[:, heads_kv * HEAD_SIZE :].astype(BF16)
    dhidden_one = ein("sfc,df->scd", dquery, q_full)
    dhidden_one = dhidden_one + ein("sfc,df->scd", dkey, k_full)
    dhidden_one = dhidden_one + ein("sfc,df->scd", dvalue, v_full)
    stacked = jnp.concatenate(
        [
            dquery.reshape(seqs, parts, nq, span),
            dkey.reshape(seqs, parts, nk, span),
            dvalue.reshape(seqs, parts, nk, span),
        ],
        axis=2,
    )
    first_grads = scatter_all(ein("scd,sofc->odf", hidden_one, stacked).astype(BF16))
    query_grad, key_grad, value_grad = first_grads[:, :nq], first_grads[:, nq : nq + nk], first_grads[:, nq + nk :]
    dnorm_one, first_term = norm_back(dhidden_one, inputs, scale_one, gain_one)
    input_grad = dafter + dnorm_one
    gain_sums = lax.psum(jnp.stack([first_term, second_term]), ("dp", "ctx"))
    own = lax.dynamic_slice_in_dim(gain_sums, lax.axis_index("ctx") * attn_gain.shape[0], attn_gain.shape[0], axis=1)
    return (
        block_output, input_grad, own[0], query_grad, key_grad, value_grad, output_grad, own[1],
        gate_grad, up_grad, down_grad,
    )


def solution(mesh):
    three, two, one = P("dp", "ctx", None), P("dp", "ctx"), P("ctx")
    return jax.shard_map(
        body,
        mesh=mesh,
        in_specs=(three, two, three, one, two, two, two, two, one, two, two, two),
        out_specs=(three, three, one, two, two, two, two, one, two, two, two),
        check_vma=False,
    )
```

```python
import functools
import math

import jax
import jax.numpy as jnp
from jax import lax
from jax.experimental import pallas as pl
from jax.experimental.pallas import tpu as pltpu
from jax.sharding import PartitionSpec as P

HEAD_SIZE = 64
HALF = HEAD_SIZE // 2
LOW = -1e30
F32 = jnp.float32
BF16 = jnp.bfloat16


def rope_tables(first, count_items):
    place = (first + jnp.arange(count_items, dtype=jnp.int32)).astype(F32)
    freq = jnp.exp(-math.log(10000.0) * jnp.arange(HALF, dtype=jnp.int32).astype(F32) * 2.0 / HEAD_SIZE)
    angle = freq[:, None] * place[None, :]
    return (jnp.cos(angle), jnp.sin(angle))


def rotate_rows(field, cosine, sine):
    seqs, features, span = field.shape
    parts = field.reshape(seqs, features // HEAD_SIZE, 2, HALF, span)
    a, b = parts[:, :, 0], parts[:, :, 1]
    return jnp.stack([a * cosine - b * sine, b * cosine + a * sine], axis=2).reshape(field.shape)


def contract(left, right, axes):
    return lax.dot_general(left, right, ((axes[:1], axes[1:]), ((), ())), preferred_element_type=F32)


def side_by_side(ref, heads, tile, size):
    cut = pl.ds(tile * size, size)
    return jnp.concatenate([ref[0, g * HEAD_SIZE : (g + 1) * HEAD_SIZE, cut] for g in range(heads)], axis=1)


def allowed_keys(j, size, start, place):
    key = j * size + lax.broadcasted_iota(jnp.int32, (size, start.shape[1]), 0)
    return (key >= start) & (key <= place)


def attend_kernel(heads, size, bounds, q_ref, kv_ref, rows_ref, o_ref, lse_ref):
    seq = pl.program_id(0)
    tiles = q_ref.shape[2] // size
    for t in range(tiles):
        q = side_by_side(q_ref, heads, t, size) * BF16(HEAD_SIZE**-0.5)
        cut = pl.ds(t * size, size)
        start = jnp.concatenate([rows_ref[0, 0:1, cut]] * heads, axis=1)
        place = jnp.concatenate([rows_ref[0, 1:2, cut]] * heads, axis=1)

        def one(j, state, masked):
            top, total, acc = state
            s = contract(kv_ref[j, 0, 0, 0], q, (0, 0))
            if masked:
                s = jnp.where(allowed_keys(j, size, start, place), s, LOW)
            new = jnp.maximum(top, jnp.max(s, axis=0, keepdims=True))
            shrink = jnp.exp(top - new)
            p = jnp.exp(s - new)
            total = total * shrink + jnp.sum(p, axis=0, keepdims=True)
            acc = acc * shrink + contract(kv_ref[j, 0, 1, 0], p.astype(BF16), (1, 0))
            return (new, total, acc)

        lanes = heads * size
        state = (jnp.full((1, lanes), LOW, F32), jnp.zeros((1, lanes), F32), jnp.zeros((HEAD_SIZE, lanes), F32))
        lo, mid, diag = (bounds[3 * (seq * tiles + t) + k] for k in range(3))
        state = lax.fori_loop(lo, mid, lambda j, c: one(j, c, True), state)
        state = lax.fori_loop(mid, diag, lambda j, c: one(j, c, False), state)
        top, total, acc = one(diag, state, True)
        out = (acc / total).astype(BF16)
        lse = top + jnp.log(total)
        for g in range(heads):
            o_ref[0, g * HEAD_SIZE : (g + 1) * HEAD_SIZE, cut] = out[:, g * size : (g + 1) * size]
            lse_ref[0, 0, g : g + 1, cut] = lse[:, g * size : (g + 1) * size]


def back_kernel(heads, size, bounds, q_ref, kv_ref, rows_ref, o_ref, do_ref, lse_ref, cos_ref, sin_ref, dq_ref, dkv_ref, sums):
    seq = pl.program_id(0)
    tiles = q_ref.shape[2] // size
    sums[...] = jnp.zeros_like(sums)
    for t in range(tiles):
        q = side_by_side(q_ref, heads, t, size) * BF16(HEAD_SIZE**-0.5)
        do = side_by_side(do_ref, heads, t, size)
        o = side_by_side(o_ref, heads, t, size)
        delta = jnp.sum(do.astype(F32) * o.astype(F32), axis=0, keepdims=True)
        cut = pl.ds(t * size, size)
        start = jnp.concatenate([rows_ref[0, 0:1, cut]] * heads, axis=1)
        place = jnp.concatenate([rows_ref[0, 1:2, cut]] * heads, axis=1)
        lse = jnp.concatenate([lse_ref[0, 0, g : g + 1, cut] for g in range(heads)], axis=1)

        def one(j, dq, masked):
            k, v = kv_ref[j, 0, 0, 0], kv_ref[j, 0, 1, 0]
            p = jnp.exp(contract(k, q, (0, 0)) - lse)
            if masked:
                p = jnp.where(allowed_keys(j, size, start, place), p, 0.0)
            dp = contract(v, do, (0, 0))
            ds = (p * (dp - delta)).astype(BF16)
            sums[j, 0] += contract(q, ds, (1, 1))
            sums[j, 1] += contract(do, p.astype(BF16), (1, 1))
            return dq + contract(k, ds, (1, 0))

        dq = jnp.zeros((HEAD_SIZE, heads * size), F32)
        lo, mid, diag = (bounds[3 * (seq * tiles + t) + k] for k in range(3))
        dq = lax.fori_loop(lo, mid, lambda j, c: one(j, c, True), dq)
        dq = lax.fori_loop(mid, diag, lambda j, c: one(j, c, False), dq)
        dq = one(diag, dq, True) * (HEAD_SIZE**-0.5)
        cosine, sine = cos_ref[:, cut], sin_ref[:, cut]
        for g in range(heads):
            a = dq[:HALF, g * size : (g + 1) * size]
            b = dq[HALF:, g * size : (g + 1) * size]
            dq_ref[0, g * HEAD_SIZE : g * HEAD_SIZE + HALF, cut] = (a * cosine + b * sine).astype(BF16)
            dq_ref[0, g * HEAD_SIZE + HALF : (g + 1) * HEAD_SIZE, cut] = (b * cosine - a * sine).astype(BF16)
    for j in range(sums.shape[0]):
        for k in range(2):
            dkv_ref[j, 0, k, 0] = sums[j, k].astype(BF16)


def attention_specs(seqs, span, all_tiles, heads_kv, heads, size):
    wide = pl.BlockSpec((1, heads * HEAD_SIZE, span), lambda s, h, b: (s, h, 0))
    kv = pl.BlockSpec((all_tiles, 1, 2, 1, HEAD_SIZE, size), lambda s, h, b: (0, s, 0, h, 0, 0))
    rows = pl.BlockSpec((1, 2, span), lambda s, h, b: (s, 0, 0))
    lse = pl.BlockSpec((1, 1, heads, span), lambda s, h, b: (s, h, 0, 0))
    table = pl.BlockSpec((HALF, span), lambda s, h, b: (0, 0))
    return wide, kv, rows, lse, table


def attend(q, kv, rows, bounds, heads):
    seqs, features, span = q.shape
    all_tiles, _, _, heads_kv, _, size = kv.shape
    wide, kvs, rs, lse, _ = attention_specs(seqs, span, all_tiles, heads_kv, heads, size)
    return pl.pallas_call(
        functools.partial(attend_kernel, heads, size),
        grid_spec=pltpu.PrefetchScalarGridSpec(
            num_scalar_prefetch=1, grid=(seqs, heads_kv), in_specs=[wide, kvs, rs], out_specs=[wide, lse]
        ),
        out_shape=[jax.ShapeDtypeStruct(q.shape, BF16), jax.ShapeDtypeStruct((seqs, heads_kv, heads, span), F32)],
        compiler_params=pltpu.CompilerParams(vmem_limit_bytes=40 << 20),
        cost_estimate=pl.CostEstimate(flops=4 * seqs * features * span * span * 3, bytes_accessed=8 << 20, transcendentals=0),
        name="attend",
    )(bounds, q, kv, rows)


def attend_back(q, kv, rows, bounds, o, do, lse, cosine, sine, heads):
    seqs, features, span = q.shape
    all_tiles, _, _, heads_kv, _, size = kv.shape
    wide, kvs, rs, ls, table = attention_specs(seqs, span, all_tiles, heads_kv, heads, size)
    return pl.pallas_call(
        functools.partial(back_kernel, heads, size),
        grid_spec=pltpu.PrefetchScalarGridSpec(
            num_scalar_prefetch=1,
            grid=(seqs, heads_kv),
            in_specs=[wide, kvs, rs, wide, wide, ls, table, table],
            out_specs=[wide, kvs],
            scratch_shapes=[pltpu.VMEM((all_tiles, 2, HEAD_SIZE, size), F32)],
        ),
        out_shape=[jax.ShapeDtypeStruct(q.shape, BF16), jax.ShapeDtypeStruct(kv.shape, BF16)],
        compiler_params=pltpu.CompilerParams(vmem_limit_bytes=40 << 20),
        cost_estimate=pl.CostEstimate(flops=seqs * features * span, bytes_accessed=1 << 20, transcendentals=0),
        name="attend_back",
    )(bounds, q, kv, rows, o, do, lse, cosine, sine)


def gather_all(shard):
    whole = lax.all_gather(shard, ("ctx", "dp"), axis=0, tiled=True)
    return whole.reshape(lax.axis_size("ctx"), -1, shard.shape[1])


def scatter_all(terms):
    flat = terms.reshape(-1, terms.shape[2])
    return lax.psum_scatter(flat, ("ctx", "dp"), scatter_dimension=0, tiled=True).astype(F32)


def bits_of(axis):
    return lax.axis_size(axis).bit_length() - 1


def all_places():
    return [(axis, bit) for axis in ("ctx", "dp") for bit in reversed(range(bits_of(axis)))]


def doubling_order(flip):
    high = [("dp", bit) for bit in reversed(range(1, bits_of("dp")))]
    low = [("dp", 0)]
    across = [("ctx", bit) for bit in reversed(range(1, bits_of("ctx")))]
    return high + (across + low if flip else low + across) + [("ctx", 0)]


def partners(axis, bit):
    return [(i, i ^ (1 << bit)) for i in range(lax.axis_size(axis))]


def side_of(axis, bit):
    return (lax.axis_index(axis) >> bit) & 1


def join(mine, other, side, at):
    low = jnp.where(side == 0, mine, other)
    high = jnp.where(side == 0, other, mine)
    return jnp.stack([low, high], axis=at)


def gather_doubling(shard, flip):
    places, held, value = all_places(), [], shard
    for place in doubling_order(flip):
        other = lax.ppermute(value, place[0], partners(*place))
        at = sum(places.index(h) < places.index(place) for h in held)
        value = join(value, other, side_of(*place), at)
        held.append(place)
    return value.reshape(lax.axis_size("ctx"), -1, shard.shape[1])


def halve(value, left, place):
    at, side = left.index(place), side_of(*place)
    away = lax.dynamic_index_in_dim(value, 1 - side, at, keepdims=False)
    kept = lax.dynamic_index_in_dim(value, side, at, keepdims=False)
    left.remove(place)
    return kept + lax.ppermute(away, place[0], partners(*place))


def halve_first(terms, flip, steps):
    left, order = all_places(), doubling_order(flip)[::-1]
    value = terms.reshape((2,) * len(left) + (-1, terms.shape[2]))
    for place in order[:steps]:
        value = halve(value, left, place)
    return value


def halve_rest(value, flip, steps):
    order = doubling_order(flip)[::-1]
    left = [place for place in all_places() if place not in order[:steps]]
    for place in order[steps:]:
        value = halve(value, left, place)
    return value.astype(F32)


def earlier_blocks(own, *later):
    value, held = own, 0
    for bit in reversed(range(bits_of("ctx"))):
        pairs = partners("ctx", bit)
        if held == 0 and bit > 0:
            pairs = [(i, j) for i, j in pairs if i < j]
        other = lax.ppermute(value, "ctx", pairs)
        if held == 0:
            other, *later = lax.optimization_barrier((other, *later))
        value = join(value, other, side_of("ctx", bit), held)
        held += 1
    return (value.reshape((-1,) + own.shape), *later)


def owners_sum(blocks, *later):
    left = [("ctx", bit) for bit in reversed(range(bits_of("ctx")))]
    value = blocks.reshape((2,) * len(left) + blocks.shape[1:])
    for place in left[::-1]:
        pairs, first = partners(*place), place[1] == 0
        if len(left) == 1 and not first:
            pairs = [(i, j) for i, j in pairs if i > j]
        at, side = left.index(place), side_of(*place)
        away = lax.dynamic_index_in_dim(value, 1 - side, at, keepdims=False)
        kept = lax.dynamic_index_in_dim(value, side, at, keepdims=False)
        value = kept + lax.ppermute(away, "ctx", pairs)
        left.remove(place)
        if first:
            value, *later = lax.optimization_barrier((value, *later))
    return (value, *later)


def every_block(own):
    value = own
    for held, bit in enumerate(reversed(range(bits_of("ctx")))):
        value = join(value, lax.ppermute(value, "ctx", partners("ctx", bit)), side_of("ctx", bit), held)
    return value.reshape((-1,) + own.shape)


def sum_everywhere(value):
    for place in all_places():
        value = value + lax.ppermute(value, place[0], partners(*place))
    return value


def term_kernel(left_ref, right_ref, out_ref):
    seqs, features, _ = left_ref.shape
    lines = math.gcd(features, 192)

    def some_rows(k, carry):
        cut = pl.ds(pl.multiple_of(k * lines, lines), lines)
        total = contract(left_ref[0, cut, :], right_ref[0, 0], (1, 1))
        for s in range(1, seqs):
            total += contract(left_ref[s, cut, :], right_ref[s, 0], (1, 1))
        out_ref[0, cut, :] = total.astype(BF16)
        return carry

    lax.fori_loop(0, features // lines, some_rows, 0)


def weight_term(left, right):
    seqs, features, span = left.shape
    _, parts, columns, _ = right.shape
    return pl.pallas_call(
        term_kernel,
        grid=(parts,),
        in_specs=[
            pl.BlockSpec((seqs, features, span), lambda p: (0, 0, 0)),
            pl.BlockSpec((seqs, 1, columns, span), lambda p: (0, p, 0, 0)),
        ],
        out_specs=pl.BlockSpec((1, features, columns), lambda p: (p, 0, 0)),
        out_shape=jax.ShapeDtypeStruct((parts, features, columns), BF16),
        compiler_params=pltpu.CompilerParams(vmem_limit_bytes=24 << 20),
        cost_estimate=pl.CostEstimate(flops=2 * seqs * span * features, bytes_accessed=1 << 20, transcendentals=0),
        name="weight_term",
    )(left, right)


def ffn_kernel(nf, h_ref, ht_ref, gb_ref, after_ref, pair_ref, d_ref, y_ref, dh_ref, pg_ref, dg_ref, dfull, hid, dgate, dup, yacc):
    c = pl.program_id(0)
    count, width = h_ref.shape
    parts = d_ref.shape[0]
    nd = d_ref.shape[2]

    @pl.when(c == 0)
    def _():
        yacc[...] = after_ref[...]
        dh_ref[...] = jnp.zeros_like(dh_ref)

    dfull[...] = jnp.concatenate([d_ref[o] for o in range(parts)], axis=1)
    step = math.gcd(count, 256)

    def token_rows(r, carry):
        cut = pl.ds(pl.multiple_of(r * step, step), step)
        h, gb = h_ref[cut, :], gb_ref[cut, :]
        g, u = pair_ref[0, :, :nf], pair_ref[0, :, nf : 2 * nf]
        gate = contract(h, g, (1, 0))
        up = contract(h, u, (1, 0))
        dhid = contract(gb, dfull[...], (1, 1))
        sg = 1.0 / (1.0 + jnp.exp(-gate))
        active = gate * sg
        low = (active * up).astype(BF16)
        hid[cut, :] = low
        yacc[cut, :] += contract(low, dfull[...], (1, 0))
        dg = (dhid * up * sg * (1.0 + gate * (1.0 - sg))).astype(BF16)
        du = (dhid * active).astype(BF16)
        dgate[cut, :] = dg
        dup[cut, :] = du
        dh_ref[cut, :] += contract(dg, g, (1, 1)) + contract(du, u, (1, 1))
        return carry

    lax.fori_loop(0, count // step, token_rows, 0)
    lines = math.gcd(width, 192)

    def pair_rows(k, carry):
        cut = pl.ds(pl.multiple_of(k * lines, lines), lines)
        ht = ht_ref[cut, :]
        pg_ref[0, cut, :nf] = contract(ht, dgate[...], (1, 0)).astype(BF16)
        pg_ref[0, cut, nf:] = contract(ht, dup[...], (1, 0)).astype(BF16)
        return carry

    lax.fori_loop(0, width // lines, pair_rows, 0)
    lanes = 128 if nf % 128 == 0 else nf
    for k in range(nf // lanes):
        term = contract(hid[:, k * lanes : (k + 1) * lanes], gb_ref[...], (0, 0))
        for o in range(parts):
            dg_ref[o, k * lanes : (k + 1) * lanes, :] = term[:, o * nd : (o + 1) * nd].astype(BF16)

    @pl.when(c == parts - 1)
    def _():
        y_ref[...] = yacc[...].astype(BF16)


def feed_forward(hidden, hidden_t, grad, after, pair, down, nf):
    count, width = hidden.shape
    parts, depth, nd = down.shape
    whole = lambda *shape: pl.BlockSpec(shape, lambda c: (0,) * len(shape), pipeline_mode=pl.Buffered(1))
    return pl.pallas_call(
        functools.partial(ffn_kernel, nf),
        grid=(parts,),
        in_specs=[
            whole(count, width), whole(width, count), whole(count, width), whole(count, width),
            pl.BlockSpec((1, width, pair.shape[2]), lambda c: (c, 0, 0)),
            pl.BlockSpec((parts, nf, nd), lambda c: (0, c, 0)),
        ],
        out_specs=[
            pl.BlockSpec((count, width), lambda c: (0, 0)),
            pl.BlockSpec((count, width), lambda c: (0, 0)),
            pl.BlockSpec((1, width, 2 * nf), lambda c: (c, 0, 0)),
            pl.BlockSpec((parts, nf, nd), lambda c: (0, c, 0)),
        ],
        out_shape=[
            jax.ShapeDtypeStruct((count, width), BF16),
            jax.ShapeDtypeStruct((count, width), F32),
            jax.ShapeDtypeStruct((parts, width, 2 * nf), BF16),
            jax.ShapeDtypeStruct((parts, depth, nd), BF16),
        ],
        scratch_shapes=[
            pltpu.VMEM((nf, width), BF16), pltpu.VMEM((count, nf), BF16), pltpu.VMEM((count, nf), BF16),
            pltpu.VMEM((count, nf), BF16), pltpu.VMEM((count, width), F32),
        ],
        compiler_params=pltpu.CompilerParams(vmem_limit_bytes=58 << 20),
        cost_estimate=pl.CostEstimate(flops=18 * count * width * depth, bytes_accessed=60 << 20, transcendentals=0),
        name="feed_forward",
    )(hidden, hidden_t, grad, after, pair, down)


def norm_back(dnorm, value, scale, gain):
    dgain = jnp.sum(dnorm * value * scale, axis=(0, 1))
    scaled = dnorm * gain
    dvalue = scale * (scaled - value * scale * scale * jnp.mean(scaled * value, axis=-1, keepdims=True))
    return (dvalue, dgain)


def ein(form, left, right):
    return jnp.einsum(form, left, right, preferred_element_type=F32)


def columns_of(blocks):
    return blocks.transpose(1, 0, 2).reshape(blocks.shape[1], -1)


def body(
    tokens, segments, cotangent, attn_gain, query_weight, key_matrix, value_matrix, output_weight, second_gain,
    gate_weight, up_weight, down_weight,
):
    parts = lax.axis_size("ctx")
    seqs, span, width = tokens.shape
    nq, nk = query_weight.shape[1], key_matrix.shape[1]
    nf = gate_weight.shape[1]
    heads_kv = nk * parts // HEAD_SIZE
    heads_q = nq * parts // HEAD_SIZE
    heads = heads_q // heads_kv
    size = math.gcd(span, 256)
    tiles = span // size

    gains = every_block(jnp.stack([attn_gain, second_gain])).transpose(1, 0, 2).reshape(2, width).astype(F32)
    segs_all = every_block(segments).transpose(1, 0, 2).reshape(seqs, parts * span)
    pair_shard = jnp.concatenate([gate_weight, up_weight, output_weight], axis=1)
    down = gather_all(down_weight)
    q_blocks = gather_doubling(query_weight, False)
    kv_blocks = gather_doubling(jnp.concatenate([key_matrix, value_matrix], axis=1), True)
    gain_one, gain_two = gains[0], gains[1]

    k_full = columns_of(kv_blocks[:, :, :nk])
    v_full = columns_of(kv_blocks[:, :, nk:])

    first = lax.axis_index("ctx") * span
    cosine, sine = rope_tables(first, span)
    place = first + jnp.arange(span, dtype=jnp.int32)
    start = jnp.sum((segs_all[:, None, :] < segments[:, :, None]).astype(jnp.int32), axis=2)
    rows = jnp.stack([start, jnp.broadcast_to(place[None], start.shape)], axis=1)
    diag = place[::size] // size
    lo = start[:, ::size] // size
    mid = jnp.minimum((start[:, size - 1 :: size] + size - 1) // size, diag[None])
    bounds = jnp.stack([lo, mid, jnp.broadcast_to(diag[None], lo.shape)], axis=2).reshape(-1)

    inputs = tokens.astype(F32)
    scale_one = lax.rsqrt(jnp.mean(inputs * inputs, axis=-1, keepdims=True) + 1e-05)
    hidden_one = (inputs * scale_one * gain_one).astype(BF16)
    key = rotate_rows(ein("df,scd->sfc", k_full, hidden_one), cosine, sine).astype(BF16)
    value = ein("df,scd->sfc", v_full, hidden_one).astype(BF16)
    kv_own = jnp.concatenate([key, value], axis=1).reshape(seqs, 2 * heads_kv * HEAD_SIZE, tiles, size)
    kv_own = kv_own.transpose(2, 0, 1, 3)
    kv, pair_shard, q_blocks = earlier_blocks(kv_own, pair_shard, q_blocks)
    q_full = columns_of(q_blocks)
    pair = gather_all(pair_shard)
    kv = kv.reshape(parts * tiles, seqs, 2, heads_kv, HEAD_SIZE, size)
    query = rotate_rows(ein("df,scd->sfc", q_full, hidden_one), cosine, sine).astype(BF16)

    query, down = lax.optimization_barrier((query, down))
    attended, lse = attend(query, kv, rows, bounds, heads)

    o_full = columns_of(pair[:, :, 2 * nf :])
    after = inputs + ein("sfc,fd->scd", attended, o_full)
    scale_two = lax.rsqrt(jnp.mean(after * after, axis=-1, keepdims=True) + 1e-05)
    hidden_two = (after * scale_two * gain_two).astype(BF16).reshape(seqs * span, width)
    grad_low = cotangent.astype(BF16).reshape(seqs * span, width)
    block_output, dhidden_two, pair_term, down_term = feed_forward(
        hidden_two, hidden_two.T, grad_low, after.reshape(seqs * span, width), pair, down, nf
    )
    block_output = block_output.reshape(seqs, span, width)
    dhidden_two = dhidden_two.reshape(seqs, span, width)
    down_sum = halve_first(down_term, True, 1)
    pair_grads = scatter_all(pair_term)
    dnorm_two, second_term = norm_back(dhidden_two, after, scale_two, gain_two)
    dafter = cotangent + dnorm_two
    dattn = dafter.astype(BF16)
    dattn_parts = dattn.transpose(0, 2, 1).reshape(seqs, parts, width // parts, span)
    output_term = weight_term(attended, dattn_parts)
    output_sum = halve_first(output_term, True, 1)

    dattended = ein("fd,scd->sfc", o_full, dattn).astype(BF16)
    dattended, down_sum = lax.optimization_barrier((dattended, down_sum))
    dquery, dkv = attend_back(query, kv, rows, bounds, attended, dattended, lse, cosine, sine, heads)
    hidden_one_t = hidden_one.transpose(0, 2, 1)
    dkv, dquery_late = owners_sum(dkv.reshape(parts, tiles, seqs, 2 * heads_kv * HEAD_SIZE, size), dquery)
    query_sum = halve_first(weight_term(hidden_one_t, dquery_late.reshape(seqs, parts, nq, span)), True, 2)
    dkv, query_sum = lax.optimization_barrier((dkv, query_sum))
    dkv = dkv.astype(F32)
    dkv = dkv.transpose(1, 2, 0, 3).reshape(seqs, 2 * heads_kv * HEAD_SIZE, span)
    dkey = rotate_rows(dkv[:, : heads_kv * HEAD_SIZE], cosine, -sine).astype(BF16)
    dvalue = dkv[:, heads_kv * HEAD_SIZE :].astype(BF16)
    dhidden_one = ein("sfc,df->scd", dquery, q_full)
    dhidden_one = dhidden_one + ein("sfc,df->scd", dkey, k_full)
    dhidden_one = dhidden_one + ein("sfc,df->scd", dvalue, v_full)
    stacked = jnp.concatenate(
        [
            dkey.reshape(seqs, parts, nk, span),
            dvalue.reshape(seqs, parts, nk, span),
        ],
        axis=2,
    )
    stacked, pair_grads = lax.optimization_barrier((stacked, pair_grads))
    gate_grad, up_grad = pair_grads[:, :nf], pair_grads[:, nf:]
    dnorm_one, first_term = norm_back(dhidden_one, inputs, scale_one, gain_one)
    kv_term, query_sum, down_sum, output_sum, gain_terms = lax.optimization_barrier(
        (weight_term(hidden_one_t, stacked), query_sum, down_sum, output_sum, jnp.stack([first_term, second_term]))
    )
    query_grad = halve_rest(query_sum, True, 2)
    down_grad = halve_rest(down_sum, True, 1)
    output_grad = halve_rest(output_sum, True, 1)
    kv_grads = halve_rest(halve_first(kv_term, False, 1), False, 1)
    key_grad, value_grad = kv_grads[:, :nk], kv_grads[:, nk:]
    input_grad = dafter + dnorm_one
    gain_sums = sum_everywhere(gain_terms)
    own = lax.dynamic_slice_in_dim(gain_sums, lax.axis_index("ctx") * attn_gain.shape[0], attn_gain.shape[0], axis=1)
    return (
        block_output, input_grad, own[0], query_grad, key_grad, value_grad, output_grad, own[1],
        gate_grad, up_grad, down_grad,
    )


def solution(mesh):
    three, two, one = P("dp", "ctx", None), P("dp", "ctx"), P("ctx")
    return jax.shard_map(
        body,
        mesh=mesh,
        in_specs=(three, two, three, one, two, two, two, two, one, two, two, two),
        out_specs=(three, three, one, two, two, two, two, one, two, two, two),
        check_vma=False,
    )
```

```python
import functools
import math

import jax
import jax.numpy as jnp
from jax import lax
from jax.experimental import pallas as pl
from jax.experimental.pallas import tpu as pltpu
from jax.sharding import PartitionSpec as P

HEAD_SIZE = 64
HALF = HEAD_SIZE // 2
LOW = -1e30
F32 = jnp.float32
BF16 = jnp.bfloat16


def rope_tables(first, count_items):
    place = (first + jnp.arange(count_items, dtype=jnp.int32)).astype(F32)
    freq = jnp.exp(-math.log(10000.0) * jnp.arange(HALF, dtype=jnp.int32).astype(F32) * 2.0 / HEAD_SIZE)
    angle = freq[:, None] * place[None, :]
    return (jnp.cos(angle), jnp.sin(angle))


def rotate_rows(field, cosine, sine):
    seqs, features, span = field.shape
    parts = field.reshape(seqs, features // HEAD_SIZE, 2, HALF, span)
    a, b = parts[:, :, 0], parts[:, :, 1]
    return jnp.stack([a * cosine - b * sine, b * cosine + a * sine], axis=2).reshape(field.shape)


def contract(left, right, axes):
    return lax.dot_general(left, right, ((axes[:1], axes[1:]), ((), ())), preferred_element_type=F32)


def side_by_side(ref, heads, tile, size):
    cut = pl.ds(tile * size, size)
    return jnp.concatenate([ref[0, g * HEAD_SIZE : (g + 1) * HEAD_SIZE, cut] for g in range(heads)], axis=1)


def allowed_keys(j, size, start, place):
    key = j * size + lax.broadcasted_iota(jnp.int32, (size, start.shape[1]), 0)
    return (key >= start) & (key <= place)


def attend_kernel(heads, size, bounds, q_ref, kv_ref, rows_ref, o_ref, lse_ref):
    seq = pl.program_id(0)
    tiles = q_ref.shape[2] // size
    for t in range(tiles):
        q = side_by_side(q_ref, heads, t, size) * BF16(HEAD_SIZE**-0.5)
        cut = pl.ds(t * size, size)
        start = jnp.concatenate([rows_ref[0, 0:1, cut]] * heads, axis=1)
        place = jnp.concatenate([rows_ref[0, 1:2, cut]] * heads, axis=1)

        def one(j, state, masked):
            top, total, acc = state
            s = contract(kv_ref[j, 0, 0, 0], q, (0, 0))
            if masked:
                s = jnp.where(allowed_keys(j, size, start, place), s, LOW)
            new = jnp.maximum(top, jnp.max(s, axis=0, keepdims=True))
            shrink = jnp.exp(top - new)
            p = jnp.exp(s - new)
            total = total * shrink + jnp.sum(p, axis=0, keepdims=True)
            acc = acc * shrink + contract(kv_ref[j, 0, 1, 0], p.astype(BF16), (1, 0))
            return (new, total, acc)

        lanes = heads * size
        state = (jnp.full((1, lanes), LOW, F32), jnp.zeros((1, lanes), F32), jnp.zeros((HEAD_SIZE, lanes), F32))
        lo, mid, diag = (bounds[3 * (seq * tiles + t) + k] for k in range(3))
        state = lax.fori_loop(lo, mid, lambda j, c: one(j, c, True), state)
        state = lax.fori_loop(mid, diag, lambda j, c: one(j, c, False), state)
        top, total, acc = one(diag, state, True)
        out = (acc / total).astype(BF16)
        lse = top + jnp.log(total)
        for g in range(heads):
            o_ref[0, g * HEAD_SIZE : (g + 1) * HEAD_SIZE, cut] = out[:, g * size : (g + 1) * size]
            lse_ref[0, 0, g : g + 1, cut] = lse[:, g * size : (g + 1) * size]


def back_kernel(heads, size, bounds, q_ref, kv_ref, rows_ref, o_ref, do_ref, lse_ref, cos_ref, sin_ref, dq_ref, dkv_ref, sums):
    seq = pl.program_id(0)
    tiles = q_ref.shape[2] // size
    sums[...] = jnp.zeros_like(sums)
    for t in range(tiles):
        q = side_by_side(q_ref, heads, t, size) * BF16(HEAD_SIZE**-0.5)
        do = side_by_side(do_ref, heads, t, size)
        o = side_by_side(o_ref, heads, t, size)
        delta = jnp.sum(do.astype(F32) * o.astype(F32), axis=0, keepdims=True)
        cut = pl.ds(t * size, size)
        start = jnp.concatenate([rows_ref[0, 0:1, cut]] * heads, axis=1)
        place = jnp.concatenate([rows_ref[0, 1:2, cut]] * heads, axis=1)
        lse = jnp.concatenate([lse_ref[0, 0, g : g + 1, cut] for g in range(heads)], axis=1)

        def one(j, dq, masked):
            k, v = kv_ref[j, 0, 0, 0], kv_ref[j, 0, 1, 0]
            p = jnp.exp(contract(k, q, (0, 0)) - lse)
            if masked:
                p = jnp.where(allowed_keys(j, size, start, place), p, 0.0)
            dp = contract(v, do, (0, 0))
            ds = (p * (dp - delta)).astype(BF16)
            sums[j, 0] += contract(q, ds, (1, 1))
            sums[j, 1] += contract(do, p.astype(BF16), (1, 1))
            return dq + contract(k, ds, (1, 0))

        dq = jnp.zeros((HEAD_SIZE, heads * size), F32)
        lo, mid, diag = (bounds[3 * (seq * tiles + t) + k] for k in range(3))
        dq = lax.fori_loop(lo, mid, lambda j, c: one(j, c, True), dq)
        dq = lax.fori_loop(mid, diag, lambda j, c: one(j, c, False), dq)
        dq = one(diag, dq, True) * (HEAD_SIZE**-0.5)
        cosine, sine = cos_ref[:, cut], sin_ref[:, cut]
        for g in range(heads):
            a = dq[:HALF, g * size : (g + 1) * size]
            b = dq[HALF:, g * size : (g + 1) * size]
            dq_ref[0, g * HEAD_SIZE : g * HEAD_SIZE + HALF, cut] = (a * cosine + b * sine).astype(BF16)
            dq_ref[0, g * HEAD_SIZE + HALF : (g + 1) * HEAD_SIZE, cut] = (b * cosine - a * sine).astype(BF16)
    for j in range(sums.shape[0]):
        for k in range(2):
            dkv_ref[j, 0, k, 0] = sums[j, k].astype(BF16)


def attention_specs(seqs, span, all_tiles, heads_kv, heads, size):
    wide = pl.BlockSpec((1, heads * HEAD_SIZE, span), lambda s, h, b: (s, h, 0))
    kv = pl.BlockSpec((all_tiles, 1, 2, 1, HEAD_SIZE, size), lambda s, h, b: (0, s, 0, h, 0, 0))
    rows = pl.BlockSpec((1, 2, span), lambda s, h, b: (s, 0, 0))
    lse = pl.BlockSpec((1, 1, heads, span), lambda s, h, b: (s, h, 0, 0))
    table = pl.BlockSpec((HALF, span), lambda s, h, b: (0, 0))
    return wide, kv, rows, lse, table


def attend(q, kv, rows, bounds, heads):
    seqs, features, span = q.shape
    all_tiles, _, _, heads_kv, _, size = kv.shape
    wide, kvs, rs, lse, _ = attention_specs(seqs, span, all_tiles, heads_kv, heads, size)
    return pl.pallas_call(
        functools.partial(attend_kernel, heads, size),
        grid_spec=pltpu.PrefetchScalarGridSpec(
            num_scalar_prefetch=1, grid=(seqs, heads_kv), in_specs=[wide, kvs, rs], out_specs=[wide, lse]
        ),
        out_shape=[jax.ShapeDtypeStruct(q.shape, BF16), jax.ShapeDtypeStruct((seqs, heads_kv, heads, span), F32)],
        compiler_params=pltpu.CompilerParams(vmem_limit_bytes=40 << 20),
        cost_estimate=pl.CostEstimate(flops=4 * seqs * features * span * span * 3, bytes_accessed=8 << 20, transcendentals=0),
        name="attend",
    )(bounds, q, kv, rows)


def attend_back(q, kv, rows, bounds, o, do, lse, cosine, sine, heads):
    seqs, features, span = q.shape
    all_tiles, _, _, heads_kv, _, size = kv.shape
    wide, kvs, rs, ls, table = attention_specs(seqs, span, all_tiles, heads_kv, heads, size)
    return pl.pallas_call(
        functools.partial(back_kernel, heads, size),
        grid_spec=pltpu.PrefetchScalarGridSpec(
            num_scalar_prefetch=1,
            grid=(seqs, heads_kv),
            in_specs=[wide, kvs, rs, wide, wide, ls, table, table],
            out_specs=[wide, kvs],
            scratch_shapes=[pltpu.VMEM((all_tiles, 2, HEAD_SIZE, size), F32)],
        ),
        out_shape=[jax.ShapeDtypeStruct(q.shape, BF16), jax.ShapeDtypeStruct(kv.shape, BF16)],
        compiler_params=pltpu.CompilerParams(vmem_limit_bytes=40 << 20),
        cost_estimate=pl.CostEstimate(flops=seqs * features * span, bytes_accessed=1 << 20, transcendentals=0),
        name="attend_back",
    )(bounds, q, kv, rows, o, do, lse, cosine, sine)


def gather_all(shard):
    whole = lax.all_gather(shard, ("ctx", "dp"), axis=0, tiled=True)
    return whole.reshape(lax.axis_size("ctx"), -1, shard.shape[1])


def scatter_all(terms):
    flat = terms.reshape(-1, terms.shape[2])
    return lax.psum_scatter(flat, ("ctx", "dp"), scatter_dimension=0, tiled=True).astype(F32)


def bits_of(axis):
    return lax.axis_size(axis).bit_length() - 1


def all_places():
    return [(axis, bit) for axis in ("ctx", "dp") for bit in reversed(range(bits_of(axis)))]


def doubling_order(flip):
    high = [("dp", bit) for bit in reversed(range(1, bits_of("dp")))]
    low = [("dp", 0)]
    across = [("ctx", bit) for bit in reversed(range(1, bits_of("ctx")))]
    return high + (across + low if flip else low + across) + [("ctx", 0)]


def partners(axis, bit):
    return [(i, i ^ (1 << bit)) for i in range(lax.axis_size(axis))]


def side_of(axis, bit):
    return (lax.axis_index(axis) >> bit) & 1


def join(mine, other, side, at):
    low = jnp.where(side == 0, mine, other)
    high = jnp.where(side == 0, other, mine)
    return jnp.stack([low, high], axis=at)


def gather_doubling(shard, flip):
    places, held, value = all_places(), [], shard
    for place in doubling_order(flip):
        other = lax.ppermute(value, place[0], partners(*place))
        at = sum(places.index(h) < places.index(place) for h in held)
        value = join(value, other, side_of(*place), at)
        held.append(place)
    return value.reshape(lax.axis_size("ctx"), -1, shard.shape[1])


def halve(value, left, place):
    at, side = left.index(place), side_of(*place)
    away = lax.dynamic_index_in_dim(value, 1 - side, at, keepdims=False)
    kept = lax.dynamic_index_in_dim(value, side, at, keepdims=False)
    left.remove(place)
    return kept + lax.ppermute(away, place[0], partners(*place))


def halve_first(terms, flip, steps):
    left, order = all_places(), doubling_order(flip)[::-1]
    value = terms.reshape((2,) * len(left) + (-1, terms.shape[2]))
    for place in order[:steps]:
        value = halve(value, left, place)
    return value


def halve_on(value, flip, begin, end):
    order = doubling_order(flip)[::-1]
    left = [place for place in all_places() if place not in order[:begin]]
    for place in order[begin:end]:
        value = halve(value, left, place)
    return value


def halve_rest(value, flip, steps):
    return halve_on(value, flip, steps, len(all_places())).astype(F32)


def earlier_blocks(own, *later):
    value, held = own, 0
    for bit in reversed(range(bits_of("ctx"))):
        pairs = partners("ctx", bit)
        if held == 0 and bit > 0:
            pairs = [(i, j) for i, j in pairs if i < j]
        other = lax.ppermute(value, "ctx", pairs)
        if held == 0:
            other, *later = lax.optimization_barrier((other, *later))
        value = join(value, other, side_of("ctx", bit), held)
        held += 1
    return (value.reshape((-1,) + own.shape), *later)


def owners_sum(blocks, *later):
    left = [("ctx", bit) for bit in reversed(range(bits_of("ctx")))]
    value = blocks.reshape((2,) * len(left) + blocks.shape[1:])
    for place in left[::-1]:
        pairs, first = partners(*place), place[1] == 0
        if len(left) == 1 and not first:
            pairs = [(i, j) for i, j in pairs if i > j]
        at, side = left.index(place), side_of(*place)
        away = lax.dynamic_index_in_dim(value, 1 - side, at, keepdims=False)
        kept = lax.dynamic_index_in_dim(value, side, at, keepdims=False)
        value = kept + lax.ppermute(away, "ctx", pairs)
        left.remove(place)
        if first:
            value, *later = lax.optimization_barrier((value, *later))
    return (value, *later)


def every_block(own):
    value = own
    for held, bit in enumerate(reversed(range(bits_of("ctx")))):
        value = join(value, lax.ppermute(value, "ctx", partners("ctx", bit)), side_of("ctx", bit), held)
    return value.reshape((-1,) + own.shape)


def sum_everywhere(value):
    for place in all_places():
        value = value + lax.ppermute(value, place[0], partners(*place))
    return value


def term_kernel(left_ref, right_ref, out_ref):
    seqs, features, _ = left_ref.shape
    lines = math.gcd(features, 192)

    def some_rows(k, carry):
        cut = pl.ds(pl.multiple_of(k * lines, lines), lines)
        total = contract(left_ref[0, cut, :], right_ref[0, 0], (1, 1))
        for s in range(1, seqs):
            total += contract(left_ref[s, cut, :], right_ref[s, 0], (1, 1))
        out_ref[0, cut, :] = total.astype(BF16)
        return carry

    lax.fori_loop(0, features // lines, some_rows, 0)


def weight_term(left, right):
    seqs, features, span = left.shape
    _, parts, columns, _ = right.shape
    return pl.pallas_call(
        term_kernel,
        grid=(parts,),
        in_specs=[
            pl.BlockSpec((seqs, features, span), lambda p: (0, 0, 0)),
            pl.BlockSpec((seqs, 1, columns, span), lambda p: (0, p, 0, 0)),
        ],
        out_specs=pl.BlockSpec((1, features, columns), lambda p: (p, 0, 0)),
        out_shape=jax.ShapeDtypeStruct((parts, features, columns), BF16),
        compiler_params=pltpu.CompilerParams(vmem_limit_bytes=24 << 20),
        cost_estimate=pl.CostEstimate(flops=2 * seqs * span * features, bytes_accessed=1 << 20, transcendentals=0),
        name="weight_term",
    )(left, right)


def ffn_kernel(nf, h_ref, ht_ref, gb_ref, after_ref, pair_ref, d_ref, y_ref, dh_ref, pg_ref, dg_ref, dfull, hid, dgate, dup, yacc):
    c = pl.program_id(0)
    count, width = h_ref.shape
    parts = d_ref.shape[0]
    nd = d_ref.shape[2]

    @pl.when(c == 0)
    def _():
        yacc[...] = after_ref[...]
        dh_ref[...] = jnp.zeros_like(dh_ref)

    dfull[...] = jnp.concatenate([d_ref[o] for o in range(parts)], axis=1)
    step = math.gcd(count, 256)

    def token_rows(r, carry):
        cut = pl.ds(pl.multiple_of(r * step, step), step)
        h, gb = h_ref[cut, :], gb_ref[cut, :]
        g, u = pair_ref[0, :, :nf], pair_ref[0, :, nf : 2 * nf]
        gate = contract(h, g, (1, 0))
        up = contract(h, u, (1, 0))
        dhid = contract(gb, dfull[...], (1, 1))
        sg = 1.0 / (1.0 + jnp.exp(-gate))
        active = gate * sg
        low = (active * up).astype(BF16)
        hid[cut, :] = low
        yacc[cut, :] += contract(low, dfull[...], (1, 0))
        dg = (dhid * up * sg * (1.0 + gate * (1.0 - sg))).astype(BF16)
        du = (dhid * active).astype(BF16)
        dgate[cut, :] = dg
        dup[cut, :] = du
        dh_ref[cut, :] += contract(dg, g, (1, 1)) + contract(du, u, (1, 1))
        return carry

    lax.fori_loop(0, count // step, token_rows, 0)
    lines = math.gcd(width, 192)

    def pair_rows(k, carry):
        cut = pl.ds(pl.multiple_of(k * lines, lines), lines)
        ht = ht_ref[cut, :]
        pg_ref[0, cut, :nf] = contract(ht, dgate[...], (1, 0)).astype(BF16)
        pg_ref[0, cut, nf:] = contract(ht, dup[...], (1, 0)).astype(BF16)
        return carry

    lax.fori_loop(0, width // lines, pair_rows, 0)
    lanes = 128 if nf % 128 == 0 else nf
    for k in range(nf // lanes):
        term = contract(hid[:, k * lanes : (k + 1) * lanes], gb_ref[...], (0, 0))
        for o in range(parts):
            dg_ref[o, k * lanes : (k + 1) * lanes, :] = term[:, o * nd : (o + 1) * nd].astype(BF16)

    @pl.when(c == parts - 1)
    def _():
        y_ref[...] = yacc[...].astype(BF16)


def feed_forward(hidden, hidden_t, grad, after, pair, down, nf):
    count, width = hidden.shape
    parts, depth, nd = down.shape
    whole = lambda *shape: pl.BlockSpec(shape, lambda c: (0,) * len(shape), pipeline_mode=pl.Buffered(1))
    return pl.pallas_call(
        functools.partial(ffn_kernel, nf),
        grid=(parts,),
        in_specs=[
            whole(count, width), whole(width, count), whole(count, width), whole(count, width),
            pl.BlockSpec((1, width, pair.shape[2]), lambda c: (c, 0, 0)),
            pl.BlockSpec((parts, nf, nd), lambda c: (0, c, 0)),
        ],
        out_specs=[
            pl.BlockSpec((count, width), lambda c: (0, 0)),
            pl.BlockSpec((count, width), lambda c: (0, 0)),
            pl.BlockSpec((1, width, 2 * nf), lambda c: (c, 0, 0)),
            pl.BlockSpec((parts, nf, nd), lambda c: (0, c, 0)),
        ],
        out_shape=[
            jax.ShapeDtypeStruct((count, width), BF16),
            jax.ShapeDtypeStruct((count, width), F32),
            jax.ShapeDtypeStruct((parts, width, 2 * nf), BF16),
            jax.ShapeDtypeStruct((parts, depth, nd), BF16),
        ],
        scratch_shapes=[
            pltpu.VMEM((nf, width), BF16), pltpu.VMEM((count, nf), BF16), pltpu.VMEM((count, nf), BF16),
            pltpu.VMEM((count, nf), BF16), pltpu.VMEM((count, width), F32),
        ],
        compiler_params=pltpu.CompilerParams(vmem_limit_bytes=58 << 20),
        cost_estimate=pl.CostEstimate(flops=18 * count * width * depth, bytes_accessed=60 << 20, transcendentals=0),
        name="feed_forward",
    )(hidden, hidden_t, grad, after, pair, down)


def norm_back(dnorm, value, scale, gain):
    dgain = jnp.sum(dnorm * value * scale, axis=(0, 1))
    scaled = dnorm * gain
    dvalue = scale * (scaled - value * scale * scale * jnp.mean(scaled * value, axis=-1, keepdims=True))
    return (dvalue, dgain)


def ein(form, left, right):
    return jnp.einsum(form, left, right, preferred_element_type=F32)


def columns_of(blocks):
    return blocks.transpose(1, 0, 2).reshape(blocks.shape[1], -1)


def body(
    tokens, segments, cotangent, attn_gain, query_weight, key_matrix, value_matrix, output_weight, second_gain,
    gate_weight, up_weight, down_weight,
):
    parts = lax.axis_size("ctx")
    seqs, span, width = tokens.shape
    nq, nk = query_weight.shape[1], key_matrix.shape[1]
    nf = gate_weight.shape[1]
    heads_kv = nk * parts // HEAD_SIZE
    heads_q = nq * parts // HEAD_SIZE
    heads = heads_q // heads_kv
    size = math.gcd(span, 256)
    tiles = span // size

    gains = every_block(jnp.stack([attn_gain, second_gain])).transpose(1, 0, 2).reshape(2, width).astype(F32)
    segs_all = every_block(segments).transpose(1, 0, 2).reshape(seqs, parts * span)
    pair_shard = jnp.concatenate([gate_weight, up_weight, output_weight], axis=1)
    down = gather_all(down_weight)
    q_blocks = gather_doubling(query_weight, False)
    kv_blocks = gather_doubling(jnp.concatenate([key_matrix, value_matrix], axis=1), True)
    gain_one, gain_two = gains[0], gains[1]

    k_full = columns_of(kv_blocks[:, :, :nk])
    v_full = columns_of(kv_blocks[:, :, nk:])

    first = lax.axis_index("ctx") * span
    cosine, sine = rope_tables(first, span)
    place = first + jnp.arange(span, dtype=jnp.int32)
    start = jnp.sum((segs_all[:, None, :] < segments[:, :, None]).astype(jnp.int32), axis=2)
    rows = jnp.stack([start, jnp.broadcast_to(place[None], start.shape)], axis=1)
    diag = place[::size] // size
    lo = start[:, ::size] // size
    mid = jnp.minimum((start[:, size - 1 :: size] + size - 1) // size, diag[None])
    bounds = jnp.stack([lo, mid, jnp.broadcast_to(diag[None], lo.shape)], axis=2).reshape(-1)

    inputs = tokens.astype(F32)
    scale_one = lax.rsqrt(jnp.mean(inputs * inputs, axis=-1, keepdims=True) + 1e-05)
    hidden_one = (inputs * scale_one * gain_one).astype(BF16)
    key = rotate_rows(ein("df,scd->sfc", k_full, hidden_one), cosine, sine).astype(BF16)
    value = ein("df,scd->sfc", v_full, hidden_one).astype(BF16)
    kv_own = jnp.concatenate([key, value], axis=1).reshape(seqs, 2 * heads_kv * HEAD_SIZE, tiles, size)
    kv_own = kv_own.transpose(2, 0, 1, 3)
    kv, pair_shard, q_blocks = earlier_blocks(kv_own, pair_shard, q_blocks)
    q_full = columns_of(q_blocks)
    pair = gather_all(pair_shard)
    kv = kv.reshape(parts * tiles, seqs, 2, heads_kv, HEAD_SIZE, size)
    query = rotate_rows(ein("df,scd->sfc", q_full, hidden_one), cosine, sine).astype(BF16)

    query, down = lax.optimization_barrier((query, down))
    attended, lse = attend(query, kv, rows, bounds, heads)

    o_full = columns_of(pair[:, :, 2 * nf :])
    after = inputs + ein("sfc,fd->scd", attended, o_full)
    scale_two = lax.rsqrt(jnp.mean(after * after, axis=-1, keepdims=True) + 1e-05)
    hidden_two = (after * scale_two * gain_two).astype(BF16).reshape(seqs * span, width)
    grad_low = cotangent.astype(BF16).reshape(seqs * span, width)
    block_output, dhidden_two, pair_term, down_term = feed_forward(
        hidden_two, hidden_two.T, grad_low, after.reshape(seqs * span, width), pair, down, nf
    )
    block_output = block_output.reshape(seqs, span, width)
    dhidden_two = dhidden_two.reshape(seqs, span, width)
    down_sum = halve_first(down_term, True, 1)
    pair_grads = scatter_all(pair_term)
    dnorm_two, second_term = norm_back(dhidden_two, after, scale_two, gain_two)
    dafter = cotangent + dnorm_two
    dattn = dafter.astype(BF16)
    dattn_parts = dattn.transpose(0, 2, 1).reshape(seqs, parts, width // parts, span)
    output_term = weight_term(attended, dattn_parts)
    output_sum = halve_first(output_term, True, 1)

    dattended = ein("fd,scd->sfc", o_full, dattn).astype(BF16)
    dattended, down_sum = lax.optimization_barrier((dattended, down_sum))
    dquery, dkv = attend_back(query, kv, rows, bounds, attended, dattended, lse, cosine, sine, heads)
    hidden_one_t = hidden_one.transpose(0, 2, 1)
    dkv, dquery_late = owners_sum(dkv.reshape(parts, tiles, seqs, 2 * heads_kv * HEAD_SIZE, size), dquery)
    query_sum = halve_first(weight_term(hidden_one_t, dquery_late.reshape(seqs, parts, nq, span)), True, 2)
    down_sum, output_sum = halve_on(down_sum, True, 1, 2), halve_on(output_sum, True, 1, 2)
    dkv, query_sum, down_sum, output_sum = lax.optimization_barrier((dkv, query_sum, down_sum, output_sum))
    dkv = dkv.astype(F32)
    dkv = dkv.transpose(1, 2, 0, 3).reshape(seqs, 2 * heads_kv * HEAD_SIZE, span)
    dkey = rotate_rows(dkv[:, : heads_kv * HEAD_SIZE], cosine, -sine).astype(BF16)
    dvalue = dkv[:, heads_kv * HEAD_SIZE :].astype(BF16)
    dhidden_one = ein("sfc,df->scd", dquery, q_full)
    dhidden_one = dhidden_one + ein("sfc,df->scd", dkey, k_full)
    dhidden_one = dhidden_one + ein("sfc,df->scd", dvalue, v_full)
    stacked = jnp.concatenate(
        [
            dkey.reshape(seqs, parts, nk, span),
            dvalue.reshape(seqs, parts, nk, span),
        ],
        axis=2,
    )
    stacked, pair_grads = lax.optimization_barrier((stacked, pair_grads))
    gate_grad, up_grad = pair_grads[:, :nf], pair_grads[:, nf:]
    dnorm_one, first_term = norm_back(dhidden_one, inputs, scale_one, gain_one)
    kv_term, query_sum, down_sum, output_sum, gain_terms = lax.optimization_barrier(
        (weight_term(hidden_one_t, stacked), query_sum, down_sum, output_sum, jnp.stack([first_term, second_term]))
    )
    query_grad = halve_rest(query_sum, True, 2)
    down_grad = halve_rest(down_sum, True, 2)
    output_grad = halve_rest(output_sum, True, 2)
    kv_grads = halve_rest(halve_first(kv_term, False, 1), False, 1)
    key_grad, value_grad = kv_grads[:, :nk], kv_grads[:, nk:]
    input_grad = dafter + dnorm_one
    gain_sums = sum_everywhere(gain_terms)
    own = lax.dynamic_slice_in_dim(gain_sums, lax.axis_index("ctx") * attn_gain.shape[0], attn_gain.shape[0], axis=1)
    return (
        block_output, input_grad, own[0], query_grad, key_grad, value_grad, output_grad, own[1],
        gate_grad, up_grad, down_grad,
    )


def solution(mesh):
    three, two, one = P("dp", "ctx", None), P("dp", "ctx"), P("ctx")
    return jax.shard_map(
        body,
        mesh=mesh,
        in_specs=(three, two, three, one, two, two, two, two, one, two, two, two),
        out_specs=(three, three, one, two, two, two, two, one, two, two, two),
        check_vma=False,
    )
```

```python
import functools
import math

import jax
import jax.numpy as jnp
from jax import lax
from jax.experimental import pallas as pl
from jax.experimental.pallas import tpu as pltpu
from jax.sharding import PartitionSpec as P

HEAD_SIZE = 64
HALF = HEAD_SIZE // 2
LOW = -1e30
F32 = jnp.float32
BF16 = jnp.bfloat16


def rope_tables(first, count_items):
    place = (first + jnp.arange(count_items, dtype=jnp.int32)).astype(F32)
    freq = jnp.exp(-math.log(10000.0) * jnp.arange(HALF, dtype=jnp.int32).astype(F32) * 2.0 / HEAD_SIZE)
    angle = freq[:, None] * place[None, :]
    return (jnp.cos(angle), jnp.sin(angle))


def rotate_rows(field, cosine, sine):
    seqs, features, span = field.shape
    parts = field.reshape(seqs, features // HEAD_SIZE, 2, HALF, span)
    a, b = parts[:, :, 0], parts[:, :, 1]
    return jnp.stack([a * cosine - b * sine, b * cosine + a * sine], axis=2).reshape(field.shape)


def contract(left, right, axes):
    return lax.dot_general(left, right, ((axes[:1], axes[1:]), ((), ())), preferred_element_type=F32)


def side_by_side(ref, heads, tile, size):
    cut = pl.ds(tile * size, size)
    return jnp.concatenate([ref[0, g * HEAD_SIZE : (g + 1) * HEAD_SIZE, cut] for g in range(heads)], axis=1)


def allowed_keys(j, size, start, place):
    key = j * size + lax.broadcasted_iota(jnp.int32, (size, start.shape[1]), 0)
    return (key >= start) & (key <= place)


def attend_kernel(heads, size, bounds, q_ref, kv_ref, rows_ref, o_ref, lse_ref):
    seq = pl.program_id(0)
    tiles = q_ref.shape[2] // size
    for t in range(tiles):
        q = side_by_side(q_ref, heads, t, size) * BF16(HEAD_SIZE**-0.5)
        cut = pl.ds(t * size, size)
        start = jnp.concatenate([rows_ref[0, 0:1, cut]] * heads, axis=1)
        place = jnp.concatenate([rows_ref[0, 1:2, cut]] * heads, axis=1)

        def one(j, state, masked):
            top, total, acc = state
            s = contract(kv_ref[j, 0, 0, 0], q, (0, 0))
            if masked:
                s = jnp.where(allowed_keys(j, size, start, place), s, LOW)
            new = jnp.maximum(top, jnp.max(s, axis=0, keepdims=True))
            shrink = jnp.exp(top - new)
            p = jnp.exp(s - new)
            total = total * shrink + jnp.sum(p, axis=0, keepdims=True)
            acc = acc * shrink + contract(kv_ref[j, 0, 1, 0], p.astype(BF16), (1, 0))
            return (new, total, acc)

        lanes = heads * size
        state = (jnp.full((1, lanes), LOW, F32), jnp.zeros((1, lanes), F32), jnp.zeros((HEAD_SIZE, lanes), F32))
        lo, mid, diag = (bounds[3 * (seq * tiles + t) + k] for k in range(3))
        state = lax.fori_loop(lo, mid, lambda j, c: one(j, c, True), state)
        state = lax.fori_loop(mid, diag, lambda j, c: one(j, c, False), state)
        top, total, acc = one(diag, state, True)
        out = (acc / total).astype(BF16)
        lse = top + jnp.log(total)
        for g in range(heads):
            o_ref[0, g * HEAD_SIZE : (g + 1) * HEAD_SIZE, cut] = out[:, g * size : (g + 1) * size]
            lse_ref[0, 0, g : g + 1, cut] = lse[:, g * size : (g + 1) * size]


def back_kernel(heads, size, bounds, q_ref, kv_ref, rows_ref, o_ref, do_ref, lse_ref, cos_ref, sin_ref, dq_ref, dkv_ref, sums):
    seq = pl.program_id(0)
    tiles = q_ref.shape[2] // size
    sums[...] = jnp.zeros_like(sums)
    for t in range(tiles):
        q = side_by_side(q_ref, heads, t, size) * BF16(HEAD_SIZE**-0.5)
        do = side_by_side(do_ref, heads, t, size)
        o = side_by_side(o_ref, heads, t, size)
        delta = jnp.sum(do.astype(F32) * o.astype(F32), axis=0, keepdims=True)
        cut = pl.ds(t * size, size)
        start = jnp.concatenate([rows_ref[0, 0:1, cut]] * heads, axis=1)
        place = jnp.concatenate([rows_ref[0, 1:2, cut]] * heads, axis=1)
        lse = jnp.concatenate([lse_ref[0, 0, g : g + 1, cut] for g in range(heads)], axis=1)

        def one(j, dq, masked):
            k, v = kv_ref[j, 0, 0, 0], kv_ref[j, 0, 1, 0]
            p = jnp.exp(contract(k, q, (0, 0)) - lse)
            if masked:
                p = jnp.where(allowed_keys(j, size, start, place), p, 0.0)
            dp = contract(v, do, (0, 0))
            ds = (p * (dp - delta)).astype(BF16)
            sums[j, 0] += contract(q, ds, (1, 1))
            sums[j, 1] += contract(do, p.astype(BF16), (1, 1))
            return dq + contract(k, ds, (1, 0))

        dq = jnp.zeros((HEAD_SIZE, heads * size), F32)
        lo, mid, diag = (bounds[3 * (seq * tiles + t) + k] for k in range(3))
        dq = lax.fori_loop(lo, mid, lambda j, c: one(j, c, True), dq)
        dq = lax.fori_loop(mid, diag, lambda j, c: one(j, c, False), dq)
        dq = one(diag, dq, True) * (HEAD_SIZE**-0.5)
        cosine, sine = cos_ref[:, cut], sin_ref[:, cut]
        for g in range(heads):
            a = dq[:HALF, g * size : (g + 1) * size]
            b = dq[HALF:, g * size : (g + 1) * size]
            dq_ref[0, g * HEAD_SIZE : g * HEAD_SIZE + HALF, cut] = (a * cosine + b * sine).astype(BF16)
            dq_ref[0, g * HEAD_SIZE + HALF : (g + 1) * HEAD_SIZE, cut] = (b * cosine - a * sine).astype(BF16)
    for j in range(sums.shape[0]):
        for k in range(2):
            dkv_ref[j, 0, k, 0] = sums[j, k].astype(BF16)


def attention_specs(seqs, span, all_tiles, heads_kv, heads, size):
    wide = pl.BlockSpec((1, heads * HEAD_SIZE, span), lambda s, h, b: (s, h, 0))
    kv = pl.BlockSpec((all_tiles, 1, 2, 1, HEAD_SIZE, size), lambda s, h, b: (0, s, 0, h, 0, 0))
    rows = pl.BlockSpec((1, 2, span), lambda s, h, b: (s, 0, 0))
    lse = pl.BlockSpec((1, 1, heads, span), lambda s, h, b: (s, h, 0, 0))
    table = pl.BlockSpec((HALF, span), lambda s, h, b: (0, 0))
    return wide, kv, rows, lse, table


def attend(q, kv, rows, bounds, heads):
    seqs, features, span = q.shape
    all_tiles, _, _, heads_kv, _, size = kv.shape
    wide, kvs, rs, lse, _ = attention_specs(seqs, span, all_tiles, heads_kv, heads, size)
    return pl.pallas_call(
        functools.partial(attend_kernel, heads, size),
        grid_spec=pltpu.PrefetchScalarGridSpec(
            num_scalar_prefetch=1, grid=(seqs, heads_kv), in_specs=[wide, kvs, rs], out_specs=[wide, lse]
        ),
        out_shape=[jax.ShapeDtypeStruct(q.shape, BF16), jax.ShapeDtypeStruct((seqs, heads_kv, heads, span), F32)],
        compiler_params=pltpu.CompilerParams(vmem_limit_bytes=40 << 20),
        cost_estimate=pl.CostEstimate(flops=4 * seqs * features * span * span * 3, bytes_accessed=8 << 20, transcendentals=0),
        name="attend",
    )(bounds, q, kv, rows)


def attend_back(q, kv, rows, bounds, o, do, lse, cosine, sine, heads):
    seqs, features, span = q.shape
    all_tiles, _, _, heads_kv, _, size = kv.shape
    wide, kvs, rs, ls, table = attention_specs(seqs, span, all_tiles, heads_kv, heads, size)
    return pl.pallas_call(
        functools.partial(back_kernel, heads, size),
        grid_spec=pltpu.PrefetchScalarGridSpec(
            num_scalar_prefetch=1,
            grid=(seqs, heads_kv),
            in_specs=[wide, kvs, rs, wide, wide, ls, table, table],
            out_specs=[wide, kvs],
            scratch_shapes=[pltpu.VMEM((all_tiles, 2, HEAD_SIZE, size), F32)],
        ),
        out_shape=[jax.ShapeDtypeStruct(q.shape, BF16), jax.ShapeDtypeStruct(kv.shape, BF16)],
        compiler_params=pltpu.CompilerParams(vmem_limit_bytes=40 << 20),
        cost_estimate=pl.CostEstimate(flops=seqs * features * span, bytes_accessed=1 << 20, transcendentals=0),
        name="attend_back",
    )(bounds, q, kv, rows, o, do, lse, cosine, sine)


def gather_all(shard):
    whole = lax.all_gather(shard, ("ctx", "dp"), axis=0, tiled=True)
    return whole.reshape(lax.axis_size("ctx"), -1, shard.shape[1])


def scatter_all(terms):
    flat = terms.reshape(-1, terms.shape[2])
    return lax.psum_scatter(flat, ("ctx", "dp"), scatter_dimension=0, tiled=True).astype(F32)


def bits_of(axis):
    return lax.axis_size(axis).bit_length() - 1


def all_places():
    return [(axis, bit) for axis in ("ctx", "dp") for bit in reversed(range(bits_of(axis)))]


def doubling_order(flip):
    high = [("dp", bit) for bit in reversed(range(1, bits_of("dp")))]
    low = [("dp", 0)]
    across = [("ctx", bit) for bit in reversed(range(1, bits_of("ctx")))]
    return high + (across + low if flip else low + across) + [("ctx", 0)]


def partners(axis, bit):
    return [(i, i ^ (1 << bit)) for i in range(lax.axis_size(axis))]


def side_of(axis, bit):
    return (lax.axis_index(axis) >> bit) & 1


def join(mine, other, side, at):
    low = jnp.where(side == 0, mine, other)
    high = jnp.where(side == 0, other, mine)
    return jnp.stack([low, high], axis=at)


def gather_doubling(shard, flip):
    places, held, value = all_places(), [], shard
    for place in doubling_order(flip):
        other = lax.ppermute(value, place[0], partners(*place))
        at = sum(places.index(h) < places.index(place) for h in held)
        value = join(value, other, side_of(*place), at)
        held.append(place)
    return value.reshape(lax.axis_size("ctx"), -1, shard.shape[1])


def halve(value, left, place):
    at, side = left.index(place), side_of(*place)
    away = lax.dynamic_index_in_dim(value, 1 - side, at, keepdims=False)
    kept = lax.dynamic_index_in_dim(value, side, at, keepdims=False)
    left.remove(place)
    return kept + lax.ppermute(away, place[0], partners(*place))


def halve_first(terms, flip, steps):
    left, order = all_places(), doubling_order(flip)[::-1]
    value = terms.reshape((2,) * len(left) + (-1, terms.shape[2]))
    for place in order[:steps]:
        value = halve(value, left, place)
    return value


def halve_on(value, flip, begin, end):
    order = doubling_order(flip)[::-1]
    left = [place for place in all_places() if place not in order[:begin]]
    for place in order[begin:end]:
        value = halve(value, left, place)
    return value


def halve_rest(value, flip, steps):
    return halve_on(value, flip, steps, len(all_places())).astype(F32)


def earlier_blocks(own, *later):
    value, held = own, 0
    for bit in reversed(range(bits_of("ctx"))):
        pairs = partners("ctx", bit)
        if held == 0 and bit > 0:
            pairs = [(i, j) for i, j in pairs if i < j]
        other = lax.ppermute(value, "ctx", pairs)
        if held == 0:
            other, *later = lax.optimization_barrier((other, *later))
        value = join(value, other, side_of("ctx", bit), held)
        held += 1
    return (value.reshape((-1,) + own.shape), *later)


def owners_sum(blocks, *later):
    left = [("ctx", bit) for bit in reversed(range(bits_of("ctx")))]
    value = blocks.reshape((2,) * len(left) + blocks.shape[1:])
    for place in left[::-1]:
        pairs, first = partners(*place), place[1] == 0
        if len(left) == 1 and not first:
            pairs = [(i, j) for i, j in pairs if i > j]
        at, side = left.index(place), side_of(*place)
        away = lax.dynamic_index_in_dim(value, 1 - side, at, keepdims=False)
        kept = lax.dynamic_index_in_dim(value, side, at, keepdims=False)
        value = kept + lax.ppermute(away, "ctx", pairs)
        left.remove(place)
        if first:
            value, *later = lax.optimization_barrier((value, *later))
    return (value, *later)


def every_block(own):
    value = own
    for held, bit in enumerate(reversed(range(bits_of("ctx")))):
        value = join(value, lax.ppermute(value, "ctx", partners("ctx", bit)), side_of("ctx", bit), held)
    return value.reshape((-1,) + own.shape)


def sum_everywhere(value):
    for place in all_places():
        value = value + lax.ppermute(value, place[0], partners(*place))
    return value


def term_kernel(left_ref, right_ref, out_ref):
    seqs, features, _ = left_ref.shape
    lines = math.gcd(features, 192)

    def some_rows(k, carry):
        cut = pl.ds(pl.multiple_of(k * lines, lines), lines)
        total = contract(left_ref[0, cut, :], right_ref[0, 0], (1, 1))
        for s in range(1, seqs):
            total += contract(left_ref[s, cut, :], right_ref[s, 0], (1, 1))
        out_ref[0, cut, :] = total.astype(BF16)
        return carry

    lax.fori_loop(0, features // lines, some_rows, 0)


def weight_term(left, right):
    seqs, features, span = left.shape
    _, parts, columns, _ = right.shape
    return pl.pallas_call(
        term_kernel,
        grid=(parts,),
        in_specs=[
            pl.BlockSpec((seqs, features, span), lambda p: (0, 0, 0)),
            pl.BlockSpec((seqs, 1, columns, span), lambda p: (0, p, 0, 0)),
        ],
        out_specs=pl.BlockSpec((1, features, columns), lambda p: (p, 0, 0)),
        out_shape=jax.ShapeDtypeStruct((parts, features, columns), BF16),
        compiler_params=pltpu.CompilerParams(vmem_limit_bytes=24 << 20),
        cost_estimate=pl.CostEstimate(flops=2 * seqs * span * features, bytes_accessed=1 << 20, transcendentals=0),
        name="weight_term",
    )(left, right)


def ffn_kernel(nf, h_ref, ht_ref, gb_ref, after_ref, pair_ref, d_ref, y_ref, dh_ref, pg_ref, dg_ref, dfull, hid, dgate, dup, yacc):
    c = pl.program_id(0)
    count, width = h_ref.shape
    parts = d_ref.shape[0]
    nd = d_ref.shape[2]

    @pl.when(c == 0)
    def _():
        yacc[...] = after_ref[...]
        dh_ref[...] = jnp.zeros_like(dh_ref)

    dfull[...] = jnp.concatenate([d_ref[o] for o in range(parts)], axis=1)
    step = math.gcd(count, 256)

    def token_rows(r, carry):
        cut = pl.ds(pl.multiple_of(r * step, step), step)
        h, gb = h_ref[cut, :], gb_ref[cut, :]
        g, u = pair_ref[0, :, :nf], pair_ref[0, :, nf : 2 * nf]
        gate = contract(h, g, (1, 0))
        up = contract(h, u, (1, 0))
        dhid = contract(gb, dfull[...], (1, 1))
        sg = 1.0 / (1.0 + jnp.exp(-gate))
        active = gate * sg
        low = (active * up).astype(BF16)
        hid[cut, :] = low
        yacc[cut, :] += contract(low, dfull[...], (1, 0))
        dg = (dhid * up * sg * (1.0 + gate * (1.0 - sg))).astype(BF16)
        du = (dhid * active).astype(BF16)
        dgate[cut, :] = dg
        dup[cut, :] = du
        dh_ref[cut, :] += contract(dg, g, (1, 1)) + contract(du, u, (1, 1))
        return carry

    lax.fori_loop(0, count // step, token_rows, 0)
    lines = math.gcd(width, 192)

    def pair_rows(k, carry):
        cut = pl.ds(pl.multiple_of(k * lines, lines), lines)
        ht = ht_ref[cut, :]
        pg_ref[0, cut, :nf] = contract(ht, dgate[...], (1, 0)).astype(BF16)
        pg_ref[0, cut, nf:] = contract(ht, dup[...], (1, 0)).astype(BF16)
        return carry

    lax.fori_loop(0, width // lines, pair_rows, 0)
    lanes = 128 if nf % 128 == 0 else nf
    for k in range(nf // lanes):
        term = contract(hid[:, k * lanes : (k + 1) * lanes], gb_ref[...], (0, 0))
        for o in range(parts):
            dg_ref[o, k * lanes : (k + 1) * lanes, :] = term[:, o * nd : (o + 1) * nd].astype(BF16)

    @pl.when(c == parts - 1)
    def _():
        y_ref[...] = yacc[...].astype(BF16)


def feed_forward(hidden, hidden_t, grad, after, pair, down, nf):
    count, width = hidden.shape
    parts, depth, nd = down.shape
    whole = lambda *shape: pl.BlockSpec(shape, lambda c: (0,) * len(shape), pipeline_mode=pl.Buffered(1))
    return pl.pallas_call(
        functools.partial(ffn_kernel, nf),
        grid=(parts,),
        in_specs=[
            whole(count, width), whole(width, count), whole(count, width), whole(count, width),
            pl.BlockSpec((1, width, pair.shape[2]), lambda c: (c, 0, 0)),
            pl.BlockSpec((parts, nf, nd), lambda c: (0, c, 0)),
        ],
        out_specs=[
            pl.BlockSpec((count, width), lambda c: (0, 0)),
            pl.BlockSpec((count, width), lambda c: (0, 0)),
            pl.BlockSpec((1, width, 2 * nf), lambda c: (c, 0, 0)),
            pl.BlockSpec((parts, nf, nd), lambda c: (0, c, 0)),
        ],
        out_shape=[
            jax.ShapeDtypeStruct((count, width), BF16),
            jax.ShapeDtypeStruct((count, width), F32),
            jax.ShapeDtypeStruct((parts, width, 2 * nf), BF16),
            jax.ShapeDtypeStruct((parts, depth, nd), BF16),
        ],
        scratch_shapes=[
            pltpu.VMEM((nf, width), BF16), pltpu.VMEM((count, nf), BF16), pltpu.VMEM((count, nf), BF16),
            pltpu.VMEM((count, nf), BF16), pltpu.VMEM((count, width), F32),
        ],
        compiler_params=pltpu.CompilerParams(vmem_limit_bytes=58 << 20),
        cost_estimate=pl.CostEstimate(flops=18 * count * width * depth, bytes_accessed=60 << 20, transcendentals=0),
        name="feed_forward",
    )(hidden, hidden_t, grad, after, pair, down)


def norm_back(dnorm, value, scale, gain):
    dgain = jnp.sum(dnorm * value * scale, axis=(0, 1))
    scaled = dnorm * gain
    dvalue = scale * (scaled - value * scale * scale * jnp.mean(scaled * value, axis=-1, keepdims=True))
    return (dvalue, dgain)


def ein(form, left, right):
    return jnp.einsum(form, left, right, preferred_element_type=F32)


def columns_of(blocks):
    return blocks.transpose(1, 0, 2).reshape(blocks.shape[1], -1)


def body(
    tokens, segments, cotangent, attn_gain, query_weight, key_matrix, value_matrix, output_weight, second_gain,
    gate_weight, up_weight, down_weight,
):
    parts = lax.axis_size("ctx")
    seqs, span, width = tokens.shape
    nq, nk = query_weight.shape[1], key_matrix.shape[1]
    nf = gate_weight.shape[1]
    heads_kv = nk * parts // HEAD_SIZE
    heads_q = nq * parts // HEAD_SIZE
    heads = heads_q // heads_kv
    size = math.gcd(span, 256)
    tiles = span // size

    gains = every_block(jnp.stack([attn_gain, second_gain])).transpose(1, 0, 2).reshape(2, width).astype(F32)
    segs_all = every_block(segments).transpose(1, 0, 2).reshape(seqs, parts * span)
    pair_shard = jnp.concatenate([gate_weight, up_weight, output_weight], axis=1)
    down = gather_all(down_weight)
    q_blocks = gather_doubling(query_weight, False)
    kv_blocks = gather_doubling(jnp.concatenate([key_matrix, value_matrix], axis=1), True)
    gain_one, gain_two = gains[0], gains[1]

    k_full = columns_of(kv_blocks[:, :, :nk])
    v_full = columns_of(kv_blocks[:, :, nk:])

    first = lax.axis_index("ctx") * span
    cosine, sine = rope_tables(first, span)
    place = first + jnp.arange(span, dtype=jnp.int32)
    start = jnp.sum((segs_all[:, None, :] < segments[:, :, None]).astype(jnp.int32), axis=2)
    rows = jnp.stack([start, jnp.broadcast_to(place[None], start.shape)], axis=1)
    diag = place[::size] // size
    lo = start[:, ::size] // size
    mid = jnp.minimum((start[:, size - 1 :: size] + size - 1) // size, diag[None])
    bounds = jnp.stack([lo, mid, jnp.broadcast_to(diag[None], lo.shape)], axis=2).reshape(-1)

    inputs = tokens.astype(F32)
    scale_one = lax.rsqrt(jnp.mean(inputs * inputs, axis=-1, keepdims=True) + 1e-05)
    hidden_one = (inputs * scale_one * gain_one).astype(BF16)
    key = rotate_rows(ein("df,scd->sfc", k_full, hidden_one), cosine, sine).astype(BF16)
    value = ein("df,scd->sfc", v_full, hidden_one).astype(BF16)
    kv_own = jnp.concatenate([key, value], axis=1).reshape(seqs, 2 * heads_kv * HEAD_SIZE, tiles, size)
    kv_own = kv_own.transpose(2, 0, 1, 3)
    kv, pair_shard, q_blocks = earlier_blocks(kv_own, pair_shard, q_blocks)
    q_full = columns_of(q_blocks)
    pair = gather_all(pair_shard)
    kv = kv.reshape(parts * tiles, seqs, 2, heads_kv, HEAD_SIZE, size)
    query = rotate_rows(ein("df,scd->sfc", q_full, hidden_one), cosine, sine).astype(BF16)

    query, down = lax.optimization_barrier((query, down))
    attended, lse = attend(query, kv, rows, bounds, heads)

    o_full = columns_of(pair[:, :, 2 * nf :])
    after = inputs + ein("sfc,fd->scd", attended, o_full)
    scale_two = lax.rsqrt(jnp.mean(after * after, axis=-1, keepdims=True) + 1e-05)
    hidden_two = (after * scale_two * gain_two).astype(BF16).reshape(seqs * span, width)
    grad_low = cotangent.astype(BF16).reshape(seqs * span, width)
    block_output, dhidden_two, pair_term, down_term = feed_forward(
        hidden_two, hidden_two.T, grad_low, after.reshape(seqs * span, width), pair, down, nf
    )
    block_output = block_output.reshape(seqs, span, width)
    dhidden_two = dhidden_two.reshape(seqs, span, width)
    down_sum = halve_first(down_term, True, 1)
    pair_grads = scatter_all(pair_term)
    dnorm_two, second_term = norm_back(dhidden_two, after, scale_two, gain_two)
    dafter = cotangent + dnorm_two
    dattn = dafter.astype(BF16)
    dattn_parts = dattn.transpose(0, 2, 1).reshape(seqs, parts, width // parts, span)
    output_term = weight_term(attended, dattn_parts)
    output_sum = halve_first(output_term, True, 1)

    dattended = ein("fd,scd->sfc", o_full, dattn).astype(BF16)
    dattended, down_sum, output_sum = lax.optimization_barrier((dattended, down_sum, output_sum))
    dquery, dkv = attend_back(query, kv, rows, bounds, attended, dattended, lse, cosine, sine, heads)
    hidden_one_t = hidden_one.transpose(0, 2, 1)
    dkv, dquery_late = owners_sum(dkv.reshape(parts, tiles, seqs, 2 * heads_kv * HEAD_SIZE, size), dquery)
    query_sum = halve_first(weight_term(hidden_one_t, dquery_late.reshape(seqs, parts, nq, span)), True, 2)
    down_sum, output_sum = halve_on(down_sum, True, 1, 2), halve_on(output_sum, True, 1, 2)
    dkv, query_sum, down_sum, output_sum = lax.optimization_barrier((dkv, query_sum, down_sum, output_sum))
    dkv = dkv.astype(F32)
    dkv = dkv.transpose(1, 2, 0, 3).reshape(seqs, 2 * heads_kv * HEAD_SIZE, span)
    dkey = rotate_rows(dkv[:, : heads_kv * HEAD_SIZE], cosine, -sine).astype(BF16)
    dvalue = dkv[:, heads_kv * HEAD_SIZE :].astype(BF16)
    dhidden_one = ein("sfc,df->scd", dquery, q_full)
    dhidden_one = dhidden_one + ein("sfc,df->scd", dkey, k_full)
    dhidden_one = dhidden_one + ein("sfc,df->scd", dvalue, v_full)
    stacked = jnp.concatenate(
        [
            dkey.reshape(seqs, parts, nk, span),
            dvalue.reshape(seqs, parts, nk, span),
        ],
        axis=2,
    )
    stacked, pair_grads = lax.optimization_barrier((stacked, pair_grads))
    gate_grad, up_grad = pair_grads[:, :nf], pair_grads[:, nf:]
    dnorm_one, first_term = norm_back(dhidden_one, inputs, scale_one, gain_one)
    kv_term, query_sum, down_sum, output_sum, gain_terms = lax.optimization_barrier(
        (weight_term(hidden_one_t, stacked), query_sum, down_sum, output_sum, jnp.stack([first_term, second_term]))
    )
    query_grad = halve_rest(query_sum, True, 2)
    down_grad = halve_rest(down_sum, True, 2)
    output_grad = halve_rest(output_sum, True, 2)
    kv_grads = halve_rest(halve_first(kv_term, False, 1), False, 1)
    key_grad, value_grad = kv_grads[:, :nk], kv_grads[:, nk:]
    input_grad = dafter + dnorm_one
    gain_sums = sum_everywhere(gain_terms)
    own = lax.dynamic_slice_in_dim(gain_sums, lax.axis_index("ctx") * attn_gain.shape[0], attn_gain.shape[0], axis=1)
    return (
        block_output, input_grad, own[0], query_grad, key_grad, value_grad, output_grad, own[1],
        gate_grad, up_grad, down_grad,
    )


def solution(mesh):
    three, two, one = P("dp", "ctx", None), P("dp", "ctx"), P("ctx")
    return jax.shard_map(
        body,
        mesh=mesh,
        in_specs=(three, two, three, one, two, two, two, two, one, two, two, two),
        out_specs=(three, three, one, two, two, two, two, one, two, two, two),
        check_vma=False,
    )
```
